256 devices in a mesh: member: 32 (over y, z), space: 8 (over x, core).
Axes of the slice: x: 4, y: 4, z: 8, core: 2. Of those that a mesh axis runs over, the one named last changes fastest.
Arguments:
- starting_fields: bfloat16 [64, 80, 32, 360], P('member', None, 'space'), may hold values from -6 to 6
- conv_weight: bfloat16 [1, 9, 80, 80], replicated, may hold values from -0.21875 to 0.21875
- norm_gain: float32 [1, 80], replicated, may hold values from 0.1 to 1.9
- weight_in: bfloat16 [1, 320, 80], replicated, may hold values from -0.625 to 0.625
- weight_out: bfloat16 [1, 80, 320], replicated, may hold values from -0.3125 to 0.3125
- obs_count: int32 [8, 32], P('space', 'member'), may hold values from 1 to 256, 4096 in all within a row
- obs_point: int32 [8, 32, 256], P('space', 'member'), may hold values from 0 to 44
- obs_channel: int32 [8, 32, 256], P('space', 'member'), may hold values from 0 to 79
- obs_value: float32 [8, 32, 256], P('space', 'member'), may hold values from -6 to 6
- obs_precision: float32 [8, 32, 256], P('space', 'member'), may hold values from 0.1 to 1
Outputs:
- analysis: bfloat16 [64, 80, 32, 360], P('member', None, 'space')
The draws below stay inside these ranges and needn't reach their ends.
Inputs may be any that keep to these rules, and one draw needn't show every extreme that they name: `obs_count`: in each band one tile has exactly 256 live slots, and the counts of a band sum to 4096.
All inputs are finite; a program needn't handle non-finite values. No bound on the sum of `obs_count` on one device may be relied on, other than what follows from the above.
Results may differ from the reference program's by a relative error of at most 0.0063.
Values may be sent and summed in bfloat16 or wider, within the bound.
No kernel may reach another device: no remote copies, remote signals or barrier semaphores. Data moves between devices by JAX's collectives and lax.ppermute only.
A program may use at most 128 MiB of HBM per device.

```python
import math
import jax
import jax.numpy as jnp
import numpy as np
from jax import lax

FIELD_VARIABLES = 80
HID = 320
LON = 360
OBS_CAP = 256
LAYERS = 1
NS_STEPS = 6
MEMBERS = 64
LAT = 32
PATCH_LOCATIONS = 45
N_MEMBER = 32
N_SPACE = 8


def set_ends(drawn, key, smallest, top_value):
    spot = [jax.random.randint(jax.random.fold_in(key, axis), (), 0, length) for axis, length in enumerate(drawn.shape)]
    widest = drawn.shape.index(max(drawn.shape))
    next_to = spot[:widest] + [(spot[widest] + 1) % drawn.shape[widest]] + spot[widest + 1:]
    return drawn.at[tuple(spot)].set(smallest).at[tuple(next_to)].set(top_value)


def shard_levels(own_key, extent, cuts, low, high):
    gain = 1.0
    for dim, blocks in cuts:
        heights = jax.random.uniform(jax.random.fold_in(jax.random.fold_in(own_key, 6), dim), (blocks,), jnp.float32, low / len(cuts), high / len(cuts))
        gain = gain * jnp.repeat(jnp.exp(heights), extent[dim] // blocks).reshape((-1,) + (1,) * (len(extent) - 1 - dim))
    return gain


def profile(amount, total, reach, skew):
    portions = [(1 << 20) // math.isqrt(standing ** skew) + 1 for standing in range(2, amount + 1)]
    surplus, holding = total - reach - (amount - 1), [1] * (amount - 1)
    while surplus > 0:
        movable = [i for i in range(amount - 1) if holding[i] < reach]
        mass, left = sum([portions[i] for i in movable]), surplus
        for i in movable:
            extra = min(reach - holding[i], max(1, left * portions[i] // mass), surplus)
            holding[i] = holding[i] + extra
            surplus = surplus - extra
    return np.array([reach] + holding)


def ragged_sizes(own_key, amount, total, limit, slope):
    if amount == 2:
        one = jax.random.randint(own_key, (), max(1, total - limit), min(limit, total - 1) + 1)
        return jnp.stack([one, total - one])
    sizes = jnp.asarray(profile(amount, total, limit, slope), jnp.int32)
    pairs = (amount - 1) // 2
    donor, receiver = sizes[1:1 + 2 * pairs:2], sizes[2:2 + 2 * pairs:2]
    margin = jnp.minimum(donor - 1, limit - receiver)
    moved = jax.random.randint(jax.random.fold_in(own_key, 1), (pairs,), 0, 1 << 20) % (margin + 1)
    sizes = sizes.at[1:1 + 2 * pairs:2].set(donor - moved).at[2:2 + 2 * pairs:2].set(receiver + moved)
    return sizes[jax.random.permutation(jax.random.fold_in(own_key, 2), amount)]


def normal_values(own_key, shape, width, bound, shards=(), kind=jnp.bfloat16):
    loudness = shard_levels(own_key, shape, shards, -0.22, 0.18) if shards else 1.0
    entries = jax.random.normal(own_key, shape, jnp.float32) * width * loudness
    return jnp.minimum(jnp.maximum(entries, -bound), bound).astype(kind)


def setup_inputs(seed: int = 0) -> dict:
    key_list = jax.random.split(jax.random.key(seed), 11)
    return {
        "starting_fields": normal_values(key_list[0], (MEMBERS, FIELD_VARIABLES, LAT, LON), 1.0, 6.0, ((0, 32), (2, 8))),
        "conv_weight": normal_values(key_list[1], (LAYERS, 9, FIELD_VARIABLES, FIELD_VARIABLES), (9 * FIELD_VARIABLES) ** -0.5, 0.21875),
        "norm_gain": jnp.clip(1.0 + 0.18 * jax.random.normal(key_list[2], (LAYERS, FIELD_VARIABLES), jnp.float32), 0.1, 1.9),
        "weight_in": normal_values(key_list[3], (LAYERS, HID, FIELD_VARIABLES), FIELD_VARIABLES ** -0.5, 0.625),
        "weight_out": normal_values(key_list[4], (LAYERS, FIELD_VARIABLES, HID), HID ** -0.5, 0.3125),
        "obs_count": jax.vmap(lambda own: ragged_sizes(own, N_MEMBER, N_MEMBER * OBS_CAP // 2, OBS_CAP, 2))(jax.random.split(key_list[5], N_SPACE)).reshape((N_SPACE, N_MEMBER)).astype(jnp.int32),
        "obs_point": set_ends(jax.random.randint(key_list[6], (N_SPACE, N_MEMBER, OBS_CAP), 0, PATCH_LOCATIONS), jax.random.fold_in(key_list[6], 1), 0, PATCH_LOCATIONS - 1).astype(jnp.int32),
        "obs_channel": set_ends(jax.random.randint(key_list[7], (N_SPACE, N_MEMBER, OBS_CAP), 0, FIELD_VARIABLES), jax.random.fold_in(key_list[7], 1), 0, FIELD_VARIABLES - 1).astype(jnp.int32),
        "obs_value": normal_values(key_list[8], (N_SPACE, N_MEMBER, OBS_CAP), 1.0, 6.0, ((0, 8), (1, 32)), jnp.float32),
        "obs_precision": jnp.clip(jnp.exp(math.log(1.0) - 2.3025851 * jax.random.uniform(key_list[9], (N_SPACE, N_MEMBER, OBS_CAP), jnp.float32) ** shard_levels(key_list[9], (N_SPACE, N_MEMBER, OBS_CAP), ((0, 8), (1, 32)), -0.2, 0.2)), 0.1, 1.0),
    }


HIGHEST_PRECISION = lax.Precision.HIGHEST
NEAR_WEIGHT = 0.5
EPSILON = 1e-06

def wide_einsum(form, left_side, right_side):
    return jnp.einsum(form, left_side.astype(jnp.float32), right_side.astype(jnp.float32), precision=HIGHEST_PRECISION)

def advance(state_now, conv_mats, gain_row, first_proj, second_proj):
    members, channels, lat_rows, lon_cols = state_now.shape
    padded = jnp.pad(state_now, ((0, 0), (0, 0), (1, 1), (0, 0)))
    summed = jnp.zeros((members, channels, lat_rows * lon_cols), jnp.float32)
    for lat_step in range(3):
        band_rows = padded[:, :, lat_step:lat_step + lat_rows, :]
        for lon_step in range(3):
            shifted = jnp.roll(band_rows, 1 - lon_step, axis=3).reshape(members, channels, lat_rows * lon_cols)
            summed = summed + wide_einsum('oi,mip->mop', conv_mats[3 * lat_step + lon_step], shifted)
    updated = state_now.reshape(members, channels, lat_rows * lon_cols).astype(jnp.float32) + summed
    normed = (updated * lax.rsqrt(lax.optimization_barrier(jnp.mean(updated * updated, axis=1, keepdims=True)) + EPSILON) * gain_row[None, :, None]).astype(jnp.bfloat16)
    hidden = jax.nn.silu(wide_einsum('hc,mcp->mhp', first_proj, normed)).astype(jnp.bfloat16)
    result = updated + wide_einsum('ch,mhp->mcp', second_proj, hidden)
    return result.astype(jnp.bfloat16).reshape(members, channels, lat_rows, lon_cols)

def sample_tile(tile_data, points_row, channel_row):
    flat_tile = tile_data.reshape(tile_data.shape[0], -1)
    return flat_tile[:, channel_row * tile_data.shape[2] + points_row].astype(jnp.float32)

def prepare(sampled, value_row, precision_row, live_count):
    average = lax.optimization_barrier(jnp.mean(sampled, axis=0))
    spread = sampled - average
    slots = jnp.arange(value_row.shape[0], dtype=jnp.int32)
    weight_matrix = jnp.where(slots < live_count, precision_row, jnp.zeros_like(precision_row))
    return (spread, weight_matrix, value_row - average)

def moments(spread, weight_matrix, innovation):
    gram = jnp.dot(spread * weight_matrix[None, :], spread.T, precision=HIGHEST_PRECISION)
    vector = jnp.dot(spread, weight_matrix * innovation, precision=HIGHEST_PRECISION)
    return (gram, vector)

def transform(gram, vector):
    sample_collection = gram.shape[0]
    identity = jnp.eye(sample_collection, dtype=jnp.float32)
    system = (sample_collection - 1.0) * identity + gram
    scale = jnp.sqrt(jnp.sum(system * system))
    root = system / scale
    inverse = identity
    for sweep_index in range(NS_STEPS):
        middle = 0.5 * (3.0 * identity - jnp.dot(inverse, root, precision=HIGHEST_PRECISION))
        root, inverse = (jnp.dot(root, middle, precision=HIGHEST_PRECISION), jnp.dot(middle, inverse, precision=HIGHEST_PRECISION))
    covariance = jnp.dot(inverse, inverse, precision=HIGHEST_PRECISION) / scale
    mean_weight = jnp.dot(covariance, vector, precision=HIGHEST_PRECISION)
    full = jnp.sqrt((sample_collection - 1.0) / scale) * inverse + mean_weight[:, None]
    return (full + (1.0 - lax.optimization_barrier(jnp.sum(full, axis=0, keepdims=True))) / sample_collection).astype(jnp.bfloat16)

def blend(tile_data, mixing):
    return wide_einsum('kcp,kl->lcp', tile_data, mixing).astype(jnp.bfloat16)

def reference(starting_fields, conv_weight, norm_gain, weight_in, weight_out, obs_count, obs_point, obs_channel, obs_value, obs_precision):

    def lone_realization(member_state):
        state_now = member_state[None]
        for depth_index in range(LAYERS):
            state_now = advance(state_now, conv_weight[depth_index], norm_gain[depth_index], weight_in[depth_index], weight_out[depth_index])
        return state_now[0]
    predict_advance = lax.map(lone_realization, starting_fields)
    sample_collection = predict_advance.shape[0]
    mesh_patches = predict_advance.reshape(sample_collection, FIELD_VARIABLES, N_SPACE, N_MEMBER, PATCH_LOCATIONS).transpose(2, 3, 0, 1, 4)
    sampled = jax.vmap(jax.vmap(sample_tile))(mesh_patches, obs_point, obs_channel)
    spread, weight_matrix, innovation = jax.vmap(jax.vmap(prepare))(sampled, obs_value, obs_precision, obs_count)
    gram, vector = jax.vmap(jax.vmap(moments))(spread, weight_matrix, innovation)
    gram = gram + NEAR_WEIGHT * (jnp.roll(gram, 1, axis=1) + jnp.roll(gram, -1, axis=1))
    vector = vector + NEAR_WEIGHT * (jnp.roll(vector, 1, axis=1) + jnp.roll(vector, -1, axis=1))
    mixing = jax.vmap(jax.vmap(transform))(gram, vector)

    def apply_band(band_pair):
        return jax.vmap(blend)(band_pair[0], band_pair[1])
    analysed = lax.map(apply_band, (mesh_patches, mixing))
    return analysed.transpose(2, 3, 0, 1, 4).reshape(sample_collection, FIELD_VARIABLES, LAT, LON)
```

```python
import jax
import jax.numpy as jnp
from jax import lax
from jax.experimental import pallas as pl
from jax.experimental.pallas import tpu as pltpu
from jax.sharding import PartitionSpec as P

NS_STEPS = 6
NEAR_WEIGHT = 0.5
EPSILON = 1e-06
MEMBERS = 64
CHANNELS = 80
ROWS = 4
LON = 360
WIDE = 384
POINTS = 45
TILES = 32
PER_ROW = 8
SUB = 8
SLOTS = CHANNELS // SUB
PACK = 512
OBS = 256
HID = 320

F32 = jnp.float32
BF16 = jnp.bfloat16


def mm(left, right):
    return jnp.dot(left, right, preferred_element_type=F32)


def mm_t(left, right):
    return lax.dot_general(left, right, (((1,), (1,)), ((), ())), preferred_element_type=F32)


def halves(value):
    high = value.astype(BF16)
    return high, (value - high.astype(F32)).astype(BF16)


def mm_split(left, right, product=mm):
    left_high, left_low = halves(left)
    right_high, right_low = halves(right)
    return product(left_high, right_high) + (
        product(left_high, right_low) + product(left_low, right_high)
    )


def pieces(source, target, length):
    found = []
    done = 0
    while done < length:
        a, b = source + done, target + done
        step = min(length - done, 128 - a % 128, 128 - b % 128)
        found.append((a // 128, b // 128, (b - a) % 128, b % 128, b % 128 + step))
        done += step
    return found


def move(value, shift):
    return pltpu.roll(value, shift, 1) if shift else value


def forecast_kernel(x_ref, low_ref, high_ref, conv_ref, gain_ref, first_ref, second_ref, out_ref, held):
    conv = jnp.concatenate(
        [conv_ref[0, 3 * a : 3 * a + 3].reshape(3 * CHANNELS, CHANNELS) for a in range(3)], axis=1
    )
    first = first_ref[0]
    second = second_ref[0]
    gain = gain_ref[...]
    lane = lax.broadcasted_iota(jnp.int32, (CHANNELS, 128), 1)

    def row(m, r):
        if r < 0:
            return low_ref[m]
        if r >= ROWS:
            return high_ref[m]
        return x_ref[m, r]

    for m in range(2):
        for h in range(2):
            rows = [row(m, 2 * h + d) for d in range(-1, 3)]
            stacked = jnp.concatenate(
                [jnp.concatenate([rows[a], rows[a + 1]], axis=1) for a in range(3)], axis=0
            )
            taps = mm(conv, stacked)
            parts = []
            for d in range(2):
                at = WIDE * d
                west = taps[:CHANNELS, at : at + WIDE]
                here = taps[CHANNELS : 2 * CHANNELS, at : at + WIDE]
                east = taps[2 * CHANNELS :, at : at + WIDE]
                end = (LON - 1) % 128
                first_wrap = move(west[:, 256:], 128 - end)
                last_wrap = move(east[:, :128], end)
                west = pltpu.roll(west, 1, 1)
                east = pltpu.roll(east, WIDE - 1, 1)
                west = jnp.concatenate([jnp.where(lane == 0, first_wrap, west[:, :128]), west[:, 128:]], axis=1)
                east = jnp.concatenate([east[:, :256], jnp.where(lane == end, last_wrap, east[:, 256:])], axis=1)
                parts.append(rows[d + 1].astype(F32) + (here + west + east))
            updated = jnp.concatenate(parts, axis=1)
            power = jnp.sum(updated * updated, axis=0, keepdims=True) * (1.0 / CHANNELS)
            normed = (updated * lax.rsqrt(power + EPSILON) * gain).astype(BF16)
            hidden = mm(first, normed)
            hidden = (hidden * (0.5 + 0.5 * jnp.tanh(0.5 * hidden))).astype(BF16)
            result = updated + mm(second, hidden)
            held[2 * h, m] = result[:, :WIDE]
            held[2 * h + 1, m] = result[:, WIDE:]

    spot = lax.broadcasted_iota(jnp.int32, (2 * SUB, 128), 1)

    @pl.loop(0, ROWS)
    def _(r):
        for j in range(PER_ROW):
            packed = [jnp.zeros((2 * SUB, 128), F32) for _ in range(PACK // 128)]
            for s in range(SLOTS):
                for a, b, shift, start, stop in pieces(j * POINTS, s * POINTS, POINTS):
                    both = held[r, :, s * SUB : (s + 1) * SUB, a * 128 : (a + 1) * 128]
                    both = move(both.reshape(2 * SUB, 128), shift)
                    packed[b] = jnp.where((spot >= start) & (spot < stop), both, packed[b])
            at = pl.multiple_of((r * PER_ROW + j) * 2 * SUB, 2 * SUB)
            out_ref[pl.ds(at, 2 * SUB), :] = jnp.concatenate(packed, axis=1).astype(BF16)


def observe_kernel(count_ref, tile_ref, point_ref, channel_ref, value_ref, precision_ref, out_ref):
    channel = channel_ref[...]
    lane = (channel // SUB) * POINTS + point_ref[...]
    place = lax.broadcasted_iota(jnp.int32, (PACK, OBS), 0)
    chosen = jnp.where(place == lane, 1.0, 0.0).astype(BF16)
    found = mm(tile_ref[...], chosen)
    found = jnp.where(place % SUB == channel % SUB, found, 0.0)
    sampled = jnp.sum(found.reshape(MEMBERS, SUB, OBS), axis=1)
    average = jnp.sum(sampled, axis=0, keepdims=True) * (1.0 / MEMBERS)
    spread = sampled - average
    slots = lax.broadcasted_iota(jnp.int32, (1, OBS), 1)
    weight = jnp.where(slots < count_ref[0, 0], precision_ref[...], 0.0)
    innovation = value_ref[...] - average
    out_ref[:, :MEMBERS] = mm_split(spread * weight, spread, mm_t)
    out_ref[:, MEMBERS : MEMBERS + 1] = jnp.sum(spread * (weight * innovation), axis=1, keepdims=True)
    out_ref[:, MEMBERS + 1 :] = jnp.zeros((MEMBERS, 128 - MEMBERS - 1), F32)


def blend_kernel(own_ref, before_ref, after_ref, tile_ref, out_ref):
    total = own_ref[...] + NEAR_WEIGHT * (before_ref[...] + after_ref[...])
    gram = total[:, :MEMBERS]
    vector = total[:, MEMBERS : MEMBERS + 1]
    identity = jnp.where(
        lax.broadcasted_iota(jnp.int32, (MEMBERS, MEMBERS), 0)
        == lax.broadcasted_iota(jnp.int32, (MEMBERS, MEMBERS), 1),
        1.0,
        0.0,
    )
    system = (MEMBERS - 1.0) * identity + gram
    squares = jnp.sum(jnp.sum(system * system, axis=0, keepdims=True), axis=1, keepdims=True)
    scale = jnp.sqrt(squares)
    root = system / scale
    middle = 1.5 * identity - 0.5 * root
    root = mm_split(root, middle)
    inverse = middle
    for sweep in range(1, NS_STEPS):
        middle = 1.5 * identity - 0.5 * mm_split(inverse, root)
        if sweep < NS_STEPS - 1:
            root = mm_split(root, middle)
        inverse = mm_split(middle, inverse)
    covariance = mm_split(inverse, inverse) / scale
    mean_weight = jnp.sum(covariance * vector, axis=0, keepdims=True)
    full = jnp.sqrt((MEMBERS - 1.0) / scale) * inverse + mean_weight
    mixing = full + (1.0 - jnp.sum(full, axis=1, keepdims=True)) * (1.0 / MEMBERS)
    mixing = mixing.astype(BF16)
    spread_rows = jnp.where(
        lax.broadcasted_iota(jnp.int32, (PACK, MEMBERS), 0) // SUB
        == lax.broadcasted_iota(jnp.int32, (PACK, MEMBERS), 1),
        1.0,
        0.0,
    ).astype(BF16)
    spread_cols = jnp.where(
        lax.broadcasted_iota(jnp.int32, (MEMBERS, PACK), 1) // SUB
        == lax.broadcasted_iota(jnp.int32, (MEMBERS, PACK), 0),
        1.0,
        0.0,
    ).astype(BF16)
    tall = mm(spread_rows, mixing).astype(BF16)
    square = mm(tall, spread_cols)
    same = (
        lax.broadcasted_iota(jnp.int32, (PACK, PACK), 0) % SUB
        == lax.broadcasted_iota(jnp.int32, (PACK, PACK), 1) % SUB
    )
    square = jnp.where(same, square, 0.0).astype(BF16)
    out_ref[...] = mm(square, tile_ref[...]).astype(BF16)


def unpack_kernel(in_ref, out_ref):
    spot = lax.broadcasted_iota(jnp.int32, (2 * SUB, 128), 1)

    @pl.loop(0, ROWS)
    def _(r):
        for pair in range(SLOTS // 2):
            lines = []
            for s in (2 * pair, 2 * pair + 1):
                line = [jnp.zeros((2 * SUB, 128), F32) for _ in range(WIDE // 128)]
                for j in range(PER_ROW):
                    at = pl.multiple_of((r * PER_ROW + j) * 2 * SUB, 2 * SUB)
                    for a, b, shift, start, stop in pieces(s * POINTS, j * POINTS, POINTS):
                        both = in_ref[pl.ds(at, 2 * SUB), a * 128 : (a + 1) * 128].astype(F32)
                        line[b] = jnp.where((spot >= start) & (spot < stop), move(both, shift), line[b])
                lines.append(jnp.concatenate(line, axis=1))
            for m in range(2):
                joined = jnp.concatenate([line[m * SUB : (m + 1) * SUB] for line in lines], axis=0)
                out_ref[m, r, pair * 2 * SUB : (pair + 1) * 2 * SUB, :] = joined.astype(BF16)[:, :LON]


def call(kernel, out_shape, *operands, **more):
    return pl.pallas_call(
        kernel,
        out_shape=out_shape,
        compiler_params=pltpu.CompilerParams(vmem_limit_bytes=40 * 1024 * 1024),
        **more,
    )(*operands)


def body(
    starting_fields,
    conv_weight,
    norm_gain,
    weight_in,
    weight_out,
    obs_count,
    obs_point,
    obs_channel,
    obs_value,
    obs_precision,
):
    fields = jnp.pad(starting_fields.transpose(0, 2, 1, 3), ((0, 0), (0, 0), (0, 0), (0, WIDE - LON)))
    bands = lax.axis_size("space")
    north = [(i, i + 1) for i in range(bands - 1)]
    low = lax.ppermute(fields[:, ROWS - 1], "space", north)
    high = lax.ppermute(fields[:, 0], "space", [(j, i) for i, j in north])
    packed = jax.ShapeDtypeStruct((PACK, PACK), BF16)
    sent = call(
        forecast_kernel,
        packed,
        fields,
        low,
        high,
        conv_weight,
        norm_gain.reshape(CHANNELS, 1),
        weight_in,
        weight_out,
        scratch_shapes=[pltpu.VMEM((ROWS, 2, CHANNELS, WIDE), F32)],
    )

    def exchange(block):
        block = block.reshape(TILES, 2 * SUB, PACK)
        block = lax.all_to_all(block, "member", split_axis=0, concat_axis=0, tiled=True)
        return block.reshape(PACK, PACK)

    tile = exchange(sent)
    whole = pl.BlockSpec(memory_space=pltpu.VMEM)
    own = call(
        observe_kernel,
        jax.ShapeDtypeStruct((MEMBERS, 128), F32),
        obs_count,
        tile,
        obs_point[0],
        obs_channel[0],
        obs_value[0],
        obs_precision[0],
        in_specs=[pl.BlockSpec(memory_space=pltpu.SMEM)] + [whole] * 5,
    )
    around = lax.axis_size("member")
    ahead = [(i, (i + 1) % around) for i in range(around)]
    before = lax.ppermute(own, "member", ahead)
    after = lax.ppermute(own, "member", [(j, i) for i, j in ahead])
    returned = exchange(call(blend_kernel, packed, own, before, after, tile))
    result = call(unpack_kernel, jax.ShapeDtypeStruct((2, ROWS, CHANNELS, LON), BF16), returned)
    return result.transpose(0, 2, 1, 3)


def solution(mesh):
    in_specs = (
        P("member", None, "space", None),
        P(),
        P(),
        P(),
        P(),
        P("space", "member"),
        P("space", "member", None),
        P("space", "member", None),
        P("space", "member", None),
        P("space", "member", None),
    )
    out_specs = P("member", None, "space", None)
    return jax.shard_map(body, mesh=mesh, in_specs=in_specs, out_specs=out_specs, check_vma=False)
```

```python
import jax
import jax.numpy as jnp
from jax import lax
from jax.experimental import pallas as pl
from jax.experimental.pallas import tpu as pltpu
from jax.sharding import PartitionSpec as P

NS_STEPS = 6
NEAR_WEIGHT = 0.5
EPSILON = 1e-06
MEMBERS = 64
CHANNELS = 80
ROWS = 4
LON = 360
WIDE = 384
POINTS = 45
TILES = 32
PER_ROW = 8
SUB = 8
SLOTS = CHANNELS // SUB
PACK = 512
OBS = 256
HID = 320

F32 = jnp.float32
BF16 = jnp.bfloat16


def mm(left, right):
    return jnp.dot(left, right, preferred_element_type=F32)


def mm_t(left, right):
    return lax.dot_general(left, right, (((1,), (1,)), ((), ())), preferred_element_type=F32)


def halves(value):
    high = value.astype(BF16)
    return high, (value - high.astype(F32)).astype(BF16)


def mm_split(left, right, product=mm):
    left_high, left_low = halves(left)
    right_high, right_low = halves(right)
    return product(left_high, right_high) + (
        product(left_high, right_low) + product(left_low, right_high)
    )


def pieces(source, target, length):
    found = []
    done = 0
    while done < length:
        a, b = source + done, target + done
        step = min(length - done, 128 - a % 128, 128 - b % 128)
        found.append((a // 128, b // 128, (b - a) % 128, b % 128, b % 128 + step))
        done += step
    return found


def move(value, shift):
    return pltpu.roll(value, shift, 1) if shift else value


def shift_wrapped(west, here, east, lane):
    end = (LON - 1) % 128
    west_wrap = move(west[:, 256:], 128 - end)
    east_wrap = move(east[:, :128], end)
    west = pltpu.roll(west, 1, 1)
    east = pltpu.roll(east, WIDE - 1, 1)
    west = jnp.concatenate([jnp.where(lane == 0, west_wrap, west[:, :128]), west[:, 128:]], axis=1)
    east = jnp.concatenate([east[:, :256], jnp.where(lane == end, east_wrap, east[:, 256:])], axis=1)
    return here + west + east


def forecast_rows(windows, conv_ref, gain_ref, first_ref, second_ref, held):
    conv = conv_ref[...]
    first = first_ref[...]
    second = second_ref[...]
    gain = gain_ref[:, :1]
    lane = lax.broadcasted_iota(jnp.int32, (CHANNELS, 128), 1)
    for m in range(2):
        near, far = windows[m]
        stacked = jnp.concatenate(
            [jnp.concatenate([near[a], far[a]], axis=1) for a in range(3)], axis=0
        )
        taps = mm(conv, stacked)
        parts = []
        for d, window in enumerate(windows[m]):
            west, here, east = [
                taps[CHANNELS * b : CHANNELS * (b + 1), WIDE * d : WIDE * (d + 1)] for b in range(3)
            ]
            parts.append(window[1].astype(F32) + shift_wrapped(west, here, east, lane))
        updated = jnp.concatenate(parts, axis=1)
        power = jnp.sum(updated * updated, axis=0, keepdims=True) * (1.0 / CHANNELS)
        normed = (updated * lax.rsqrt(power + EPSILON) * gain).astype(BF16)
        hidden = mm(first, normed)
        hidden = (hidden * (0.5 + 0.5 * jnp.tanh(0.5 * hidden))).astype(BF16)
        result = updated + mm(second, hidden)
        held[0, m] = result[:, :WIDE]
        held[1, m] = result[:, WIDE:]


def pack_rows(held, starts, out_ref):
    spot = lax.broadcasted_iota(jnp.int32, (2 * SUB, 128), 1)
    for i, start in enumerate(starts):
        for j in range(PER_ROW):
            packed = [jnp.zeros((2 * SUB, 128), F32) for _ in range(PACK // 128)]
            for s in range(SLOTS):
                for a, b, shift, low, high in pieces(j * POINTS, s * POINTS, POINTS):
                    both = held[i, :, s * SUB : (s + 1) * SUB, a * 128 : (a + 1) * 128]
                    both = move(both.reshape(2 * SUB, 128), shift)
                    packed[b] = jnp.where((spot >= low) & (spot < high), both, packed[b])
            at = start + j * 2 * SUB
            out_ref[at : at + 2 * SUB, :] = jnp.concatenate(packed, axis=1).astype(BF16)


ROW_PACK = PER_ROW * 2 * SUB


def inner_kernel(
    x_ref,
    conv,
    gain,
    first,
    count,
    point,
    channel,
    value,
    precision,
    second_ref,
    out_ref,
    conv_ref,
    gain_ref,
    first_ref,
    obs_ref,
    held,
):
    conv_ref[...] = jnp.concatenate(
        [conv[0, 3 * a : 3 * a + 3].reshape(3 * CHANNELS, CHANNELS) for a in range(3)], axis=1
    )
    row = lax.broadcasted_iota(jnp.int32, (CHANNELS, CHANNELS), 0)
    column = lax.broadcasted_iota(jnp.int32, (CHANNELS, CHANNELS), 1)
    tall = jnp.sum(jnp.where(row == column, gain[...], 0.0), axis=1, keepdims=True)
    gain_ref[...] = jnp.broadcast_to(tall, (CHANNELS, 128))
    first_ref[...] = first[...].astype(F32).T.astype(BF16)
    slots = lax.broadcasted_iota(jnp.int32, (1, OBS), 1)
    obs_ref[0:1, :] = ((channel[...] // SUB) * POINTS + point[...]).astype(F32)
    obs_ref[1:2, :] = (channel[...] % SUB).astype(F32)
    obs_ref[2:3, :] = jnp.where(slots < count[...], precision[...], 0.0)
    obs_ref[3:4, :] = value[...]
    obs_ref[4:, :] = jnp.zeros((4, OBS), F32)
    windows = [[[x_ref[m, r + d] for d in (-1, 0, 1)] for r in (1, 2)] for m in range(2)]
    forecast_rows(windows, conv_ref, gain_ref, first_ref, second_ref, held)
    pack_rows(held, (0, ROW_PACK), out_ref)


def outer_kernel(
    odd_ref,
    x_ref,
    chip_ref,
    next_ref,
    inner_ref,
    conv_ref,
    gain_ref,
    first_ref,
    second_ref,
    out_ref,
    held,
):
    odd = odd_ref[...] == 1
    windows = []
    for m in range(2):
        low = jnp.where(odd, chip_ref[m].astype(F32), next_ref[m].astype(F32)).astype(BF16)
        high = jnp.where(odd, next_ref[m].astype(F32), chip_ref[m].astype(F32)).astype(BF16)
        windows.append([[low, x_ref[m, 0], x_ref[m, 1]], [x_ref[m, 2], x_ref[m, 3], high]])
    forecast_rows(windows, conv_ref, gain_ref, first_ref, second_ref, held)
    pack_rows(held, (0, 3 * ROW_PACK), out_ref)
    out_ref[ROW_PACK : 3 * ROW_PACK, :] = inner_ref[...]


def observe_kernel(tile_ref, obs_ref, out_ref):
    place = lax.broadcasted_iota(jnp.int32, (PACK, OBS), 0)
    lane = obs_ref[0:1, :].astype(jnp.int32)
    sub = obs_ref[1:2, :].astype(jnp.int32)
    weight = obs_ref[2:3, :]
    found = mm(tile_ref[...], jnp.where(place == lane, 1.0, 0.0).astype(BF16))
    found = jnp.where(place % SUB == sub, found, 0.0)
    sampled = jnp.sum(found.reshape(MEMBERS, SUB, OBS), axis=1)
    average = jnp.sum(sampled, axis=0, keepdims=True) * (1.0 / MEMBERS)
    spread = sampled - average
    innovation = obs_ref[3:4, :] - average
    gram = mm_split(spread * weight, spread, mm_t)
    out_ref[: MEMBERS // 2, :MEMBERS] = gram[: MEMBERS // 2]
    out_ref[: MEMBERS // 2, MEMBERS:] = gram[MEMBERS // 2 :]
    pull = jnp.broadcast_to(weight * innovation, (8, OBS))
    out_ref[MEMBERS // 2 :, :MEMBERS] = mm_split(pull, spread, mm_t)
    out_ref[MEMBERS // 2 :, MEMBERS:] = jnp.zeros((8, MEMBERS), F32)


def blend_kernel(own_ref, far_ref, near_ref, tile_ref, out_ref):
    total = own_ref[...] + NEAR_WEIGHT * (far_ref[...] + near_ref[...])
    gram = jnp.concatenate([total[: MEMBERS // 2, :MEMBERS], total[: MEMBERS // 2, MEMBERS:]], axis=0)
    vector = total[MEMBERS // 2 : MEMBERS // 2 + 1, :MEMBERS]
    identity = jnp.where(
        lax.broadcasted_iota(jnp.int32, (MEMBERS, MEMBERS), 0)
        == lax.broadcasted_iota(jnp.int32, (MEMBERS, MEMBERS), 1),
        1.0,
        0.0,
    )
    system = (MEMBERS - 1.0) * identity + gram
    squares = jnp.sum(jnp.sum(system * system, axis=0, keepdims=True), axis=1, keepdims=True)
    scale = jnp.sqrt(squares)
    root = system / scale
    middle = 1.5 * identity - 0.5 * root
    root = mm_split(root, middle)
    inverse = middle
    for sweep in range(1, NS_STEPS):
        middle = 1.5 * identity - 0.5 * mm_split(inverse, root)
        if sweep < NS_STEPS - 1:
            root = mm_split(root, middle)
        inverse = mm_split(middle, inverse)
    once = jnp.sum(inverse * vector, axis=1, keepdims=True)
    mean_weight = jnp.sum(inverse * once, axis=0, keepdims=True) / scale
    full = jnp.sqrt((MEMBERS - 1.0) / scale) * inverse + mean_weight
    mixing = full + (1.0 - jnp.sum(full, axis=1, keepdims=True)) * (1.0 / MEMBERS)
    mixing = mixing.astype(BF16)
    spread_cols = jnp.where(
        lax.broadcasted_iota(jnp.int32, (MEMBERS, PACK), 1) // SUB
        == lax.broadcasted_iota(jnp.int32, (MEMBERS, PACK), 0),
        1.0,
        0.0,
    ).astype(BF16)
    wide = mm(mixing, spread_cols)
    square = jnp.broadcast_to(wide[:, None, :], (MEMBERS, SUB, PACK)).reshape(PACK, PACK)
    same = (
        lax.broadcasted_iota(jnp.int32, (PACK, PACK), 0) % SUB
        == lax.broadcasted_iota(jnp.int32, (PACK, PACK), 1) % SUB
    )
    square = jnp.where(same, square, 0.0).astype(BF16)
    out_ref[...] = mm(square, tile_ref[...]).astype(BF16)


def unpack_kernel(in_ref, out_ref):
    spot = lax.broadcasted_iota(jnp.int32, (2 * SUB, 128), 1)

    @pl.loop(0, ROWS)
    def _(r):
        for pair in range(SLOTS // 2):
            lines = []
            for s in (2 * pair, 2 * pair + 1):
                line = [jnp.zeros((2 * SUB, 128), F32) for _ in range(WIDE // 128)]
                for j in range(PER_ROW):
                    at = pl.multiple_of((r * PER_ROW + j) * 2 * SUB, 2 * SUB)
                    for a, b, shift, start, stop in pieces(s * POINTS, j * POINTS, POINTS):
                        both = in_ref[pl.ds(at, 2 * SUB), a * 128 : (a + 1) * 128].astype(F32)
                        line[b] = jnp.where((spot >= start) & (spot < stop), move(both, shift), line[b])
                lines.append(jnp.concatenate(line, axis=1))
            for m in range(2):
                joined = jnp.concatenate([line[m * SUB : (m + 1) * SUB] for line in lines], axis=0)
                out_ref[m, r, pair * 2 * SUB : (pair + 1) * 2 * SUB, :] = joined.astype(BF16)[:, :LON]


def call(kernel, out_shape, *operands, **more):
    return pl.pallas_call(
        kernel,
        out_shape=out_shape,
        compiler_params=pltpu.CompilerParams(vmem_limit_bytes=40 * 1024 * 1024),
        **more,
    )(*operands)


def body(
    starting_fields,
    conv_weight,
    norm_gain,
    weight_in,
    weight_out,
    obs_count,
    obs_point,
    obs_channel,
    obs_value,
    obs_precision,
):
    fields = jnp.pad(starting_fields.transpose(0, 2, 1, 3), ((0, 0), (0, 0), (0, 0), (0, WIDE - LON)))
    fields = lax.optimization_barrier(fields)
    bands = lax.axis_size("space")
    odd = lax.axis_index("space") % 2
    top, bottom = fields[:, 0], fields[:, ROWS - 1]
    across = [(i, i + 1 if i % 2 else i - 1) for i in range(1, bands - 1)]
    next_row = lax.ppermute(jnp.where(odd == 1, bottom, top), "space", across)
    within = [(i, i ^ 1) for i in range(bands)]
    chip_row = lax.ppermute(jnp.where(odd == 1, top, bottom), "space", within)
    held = [pltpu.VMEM((2, 2, CHANNELS, WIDE), F32)]
    second = weight_out[0]
    inner, conv, gain, first, observations = call(
        inner_kernel,
        (
            jax.ShapeDtypeStruct((2 * ROW_PACK, PACK), BF16),
            jax.ShapeDtypeStruct((3 * CHANNELS, 3 * CHANNELS), BF16),
            jax.ShapeDtypeStruct((CHANNELS, 128), F32),
            jax.ShapeDtypeStruct((HID, CHANNELS), BF16),
            jax.ShapeDtypeStruct((8, OBS), F32),
        ),
        fields,
        conv_weight,
        norm_gain,
        weight_in[0].T,
        obs_count,
        obs_point[0],
        obs_channel[0],
        obs_value[0],
        obs_precision[0],
        second,
        scratch_shapes=held,
        cost_estimate=pl.CostEstimate(flops=400_000_000, bytes_accessed=2_000_000, transcendentals=500_000),
    )
    weights = (conv, gain, first, second)
    packed = jax.ShapeDtypeStruct((PACK, PACK), BF16)
    sent = call(
        outer_kernel, packed, odd.reshape(1, 1), fields, chip_row, next_row, inner, *weights, scratch_shapes=held
    )

    def exchange(block):
        block = block.reshape(TILES, 2 * SUB, PACK)
        block = lax.all_to_all(block, "member", split_axis=0, concat_axis=0, tiled=True)
        return block.reshape(PACK, PACK)

    tile = exchange(sent)
    own = call(observe_kernel, jax.ShapeDtypeStruct((MEMBERS // 2 + 8, 128), F32), tile, observations)
    around = lax.axis_size("member")
    far = lax.ppermute(own, "member", [(i, (i + 1 if i % 2 else i - 1) % around) for i in range(around)])
    near = lax.ppermute(own, "member", [(i, i ^ 1) for i in range(around)])
    returned = exchange(call(blend_kernel, packed, own, far, near, tile))
    result = call(unpack_kernel, jax.ShapeDtypeStruct((2, ROWS, CHANNELS, LON), BF16), returned)
    return result.transpose(0, 2, 1, 3)


def solution(mesh):
    in_specs = (
        P("member", None, "space", None),
        P(),
        P(),
        P(),
        P(),
        P("space", "member"),
        P("space", "member", None),
        P("space", "member", None),
        P("space", "member", None),
        P("space", "member", None),
    )
    out_specs = P("member", None, "space", None)
    return jax.shard_map(body, mesh=mesh, in_specs=in_specs, out_specs=out_specs, check_vma=False)
```

```python
import jax
import jax.numpy as jnp
from jax import lax
from jax.experimental import pallas as pl
from jax.experimental.pallas import tpu as pltpu
from jax.sharding import PartitionSpec as P

NS_STEPS = 6
NEAR_WEIGHT = 0.5
EPSILON = 1e-06
MEMBERS = 64
CHANNELS = 80
ROWS = 4
LON = 360
WIDE = 384
POINTS = 45
TILES = 32
PER_ROW = 8
SUB = 8
SLOTS = CHANNELS // SUB
PACK = 512
OBS = 256
HID = 320

F32 = jnp.float32
BF16 = jnp.bfloat16


def mm(left, right):
    return jnp.dot(left, right, preferred_element_type=F32)


def mm_t(left, right):
    return lax.dot_general(left, right, (((1,), (1,)), ((), ())), preferred_element_type=F32)


def halves(value):
    high = value.astype(BF16)
    return high, (value - high.astype(F32)).astype(BF16)


def mm_split(left, right, product=mm):
    left_high, left_low = halves(left)
    right_high, right_low = halves(right)
    return product(left_high, right_high) + (
        product(left_high, right_low) + product(left_low, right_high)
    )


def pieces(source, target, length):
    found = []
    done = 0
    while done < length:
        a, b = source + done, target + done
        step = min(length - done, 128 - a % 128, 128 - b % 128)
        found.append((a // 128, b // 128, (b - a) % 128, b % 128, b % 128 + step))
        done += step
    return found


def move(value, shift):
    return pltpu.roll(value, shift, 1) if shift else value


def shift_wrapped(west, here, east, lane):
    end = (LON - 1) % 128
    west_wrap = move(west[:, 256:], 128 - end)
    east_wrap = move(east[:, :128], end)
    west = pltpu.roll(west, 1, 1)
    east = pltpu.roll(east, WIDE - 1, 1)
    west = jnp.concatenate([jnp.where(lane == 0, west_wrap, west[:, :128]), west[:, 128:]], axis=1)
    east = jnp.concatenate([east[:, :256], jnp.where(lane == end, east_wrap, east[:, 256:])], axis=1)
    return here + west + east


def forecast_rows(windows, conv_ref, gain_ref, first_ref, second_ref, held):
    conv = conv_ref[...]
    first = first_ref[...]
    second = second_ref[...]
    gain = gain_ref[:, :1]
    lane = lax.broadcasted_iota(jnp.int32, (CHANNELS, 128), 1)
    for m in range(2):
        near, far = windows[m]
        stacked = jnp.concatenate(
            [jnp.concatenate([near[a], far[a]], axis=1) for a in range(3)], axis=0
        )
        taps = mm(conv, stacked)
        parts = []
        for d, window in enumerate(windows[m]):
            west, here, east = [
                taps[CHANNELS * b : CHANNELS * (b + 1), WIDE * d : WIDE * (d + 1)] for b in range(3)
            ]
            parts.append(window[1].astype(F32) + shift_wrapped(west, here, east, lane))
        updated = jnp.concatenate(parts, axis=1)
        power = jnp.sum(updated * updated, axis=0, keepdims=True) * (1.0 / CHANNELS)
        normed = (updated * lax.rsqrt(power + EPSILON) * gain).astype(BF16)
        hidden = mm(first, normed)
        hidden = (hidden * (0.5 + 0.5 * jnp.tanh(0.5 * hidden))).astype(BF16)
        result = updated + mm(second, hidden)
        held[0, m] = result[:, :WIDE]
        held[1, m] = result[:, WIDE:]


def pack_rows(held, starts, out_ref):
    spot = lax.broadcasted_iota(jnp.int32, (2 * SUB, 128), 1)
    for i, start in enumerate(starts):
        for j in range(PER_ROW):
            packed = [jnp.zeros((2 * SUB, 128), F32) for _ in range(PACK // 128)]
            for s in range(SLOTS):
                for a, b, shift, low, high in pieces(j * POINTS, s * POINTS, POINTS):
                    both = held[i, :, s * SUB : (s + 1) * SUB, a * 128 : (a + 1) * 128]
                    both = move(both.reshape(2 * SUB, 128), shift)
                    packed[b] = jnp.where((spot >= low) & (spot < high), both, packed[b])
            at = start + j * 2 * SUB
            out_ref[at : at + 2 * SUB, :] = jnp.concatenate(packed, axis=1).astype(BF16)


ROW_PACK = PER_ROW * 2 * SUB


def inner_kernel(
    x_ref,
    conv,
    gain,
    first,
    count,
    point,
    channel,
    value,
    precision,
    second_ref,
    out_ref,
    conv_ref,
    gain_ref,
    first_ref,
    obs_ref,
    held,
):
    conv_ref[...] = jnp.concatenate(
        [conv[0, 3 * a : 3 * a + 3].reshape(3 * CHANNELS, CHANNELS) for a in range(3)], axis=1
    )
    row = lax.broadcasted_iota(jnp.int32, (CHANNELS, CHANNELS), 0)
    column = lax.broadcasted_iota(jnp.int32, (CHANNELS, CHANNELS), 1)
    tall = jnp.sum(jnp.where(row == column, gain[...], 0.0), axis=1, keepdims=True)
    gain_ref[...] = jnp.broadcast_to(tall, (CHANNELS, 128))
    first_ref[...] = first[...].astype(F32).T.astype(BF16)
    slots = lax.broadcasted_iota(jnp.int32, (1, OBS), 1)
    obs_ref[0:1, :] = ((channel[...] // SUB) * POINTS + point[...]).astype(F32)
    obs_ref[1:2, :] = (channel[...] % SUB).astype(F32)
    obs_ref[2:3, :] = jnp.where(slots < count[...], precision[...], 0.0)
    obs_ref[3:4, :] = value[...]
    obs_ref[4:, :] = jnp.zeros((4, OBS), F32)
    windows = [[[x_ref[m, r + d] for d in (-1, 0, 1)] for r in (1, 2)] for m in range(2)]
    forecast_rows(windows, conv_ref, gain_ref, first_ref, second_ref, held)
    pack_rows(held, (0, ROW_PACK), out_ref)


def outer_kernel(
    odd_ref,
    x_ref,
    chip_ref,
    next_ref,
    inner_ref,
    conv_ref,
    gain_ref,
    first_ref,
    second_ref,
    out_ref,
    held,
):
    odd = odd_ref[...] == 1
    windows = []
    for m in range(2):
        low = jnp.where(odd, chip_ref[m].astype(F32), next_ref[m].astype(F32)).astype(BF16)
        high = jnp.where(odd, next_ref[m].astype(F32), chip_ref[m].astype(F32)).astype(BF16)
        windows.append([[low, x_ref[m, 0], x_ref[m, 1]], [x_ref[m, 2], x_ref[m, 3], high]])
    forecast_rows(windows, conv_ref, gain_ref, first_ref, second_ref, held)
    pack_rows(held, (0, 3 * ROW_PACK), out_ref)
    out_ref[ROW_PACK : 3 * ROW_PACK, :] = inner_ref[...]


def observe_kernel(tile_ref, obs_ref, out_ref):
    place = lax.broadcasted_iota(jnp.int32, (PACK, OBS), 0)
    lane = obs_ref[0:1, :].astype(jnp.int32)
    sub = obs_ref[1:2, :].astype(jnp.int32)
    weight = obs_ref[2:3, :]
    found = mm(tile_ref[...], jnp.where(place == lane, 1.0, 0.0).astype(BF16))
    found = jnp.where(place % SUB == sub, found, 0.0)
    sampled = jnp.sum(found.reshape(MEMBERS, SUB, OBS), axis=1)
    average = jnp.sum(sampled, axis=0, keepdims=True) * (1.0 / MEMBERS)
    spread = sampled - average
    innovation = obs_ref[3:4, :] - average
    gram = mm_split(spread * weight, spread, mm_t)
    out_ref[: MEMBERS // 2, :MEMBERS] = gram[: MEMBERS // 2]
    out_ref[: MEMBERS // 2, MEMBERS:] = gram[MEMBERS // 2 :]
    pull = jnp.broadcast_to(weight * innovation, (8, OBS))
    out_ref[MEMBERS // 2 :, :MEMBERS] = mm_split(pull, spread, mm_t)
    out_ref[MEMBERS // 2 :, MEMBERS:] = jnp.zeros((8, MEMBERS), F32)


def blend_kernel(own_ref, near_ref, far_ref, tile_ref, out_ref):
    total = own_ref[...] + NEAR_WEIGHT * (near_ref[...] + far_ref[...])
    gram = jnp.concatenate([total[: MEMBERS // 2, :MEMBERS], total[: MEMBERS // 2, MEMBERS:]], axis=0)
    vector = total[MEMBERS // 2 : MEMBERS // 2 + 1, :MEMBERS]
    identity = jnp.where(
        lax.broadcasted_iota(jnp.int32, (MEMBERS, MEMBERS), 0)
        == lax.broadcasted_iota(jnp.int32, (MEMBERS, MEMBERS), 1),
        1.0,
        0.0,
    )
    system = (MEMBERS - 1.0) * identity + gram
    squares = jnp.sum(jnp.sum(system * system, axis=0, keepdims=True), axis=1, keepdims=True)
    scale = jnp.sqrt(squares)
    root = system / scale
    middle = 1.5 * identity - 0.5 * root
    root = mm_split(root, middle)
    inverse = middle
    for sweep in range(1, NS_STEPS):
        middle = 1.5 * identity - 0.5 * mm_split(inverse, root)
        if sweep < NS_STEPS - 1:
            root = mm_split(root, middle)
        inverse = mm_split(middle, inverse)
    once = jnp.sum(inverse * vector, axis=1, keepdims=True)
    mean_weight = jnp.sum(inverse * once, axis=0, keepdims=True) / scale
    full = jnp.sqrt((MEMBERS - 1.0) / scale) * inverse + mean_weight
    mixing = full + (1.0 - jnp.sum(full, axis=1, keepdims=True)) * (1.0 / MEMBERS)
    mixing = mixing.astype(BF16)
    spread_cols = jnp.where(
        lax.broadcasted_iota(jnp.int32, (MEMBERS, PACK), 1) // SUB
        == lax.broadcasted_iota(jnp.int32, (MEMBERS, PACK), 0),
        1.0,
        0.0,
    ).astype(BF16)
    wide = mm(mixing, spread_cols)
    square = jnp.broadcast_to(wide[:, None, :], (MEMBERS, SUB, PACK)).reshape(PACK, PACK)
    same = (
        lax.broadcasted_iota(jnp.int32, (PACK, PACK), 0) % SUB
        == lax.broadcasted_iota(jnp.int32, (PACK, PACK), 1) % SUB
    )
    square = jnp.where(same, square, 0.0).astype(BF16)
    out_ref[...] = mm(square, tile_ref[...]).astype(BF16)


def unpack_kernel(in_ref, out_ref):
    spot = lax.broadcasted_iota(jnp.int32, (2 * SUB, 128), 1)

    @pl.loop(0, ROWS)
    def _(r):
        for pair in range(SLOTS // 2):
            lines = []
            for s in (2 * pair, 2 * pair + 1):
                line = [jnp.zeros((2 * SUB, 128), F32) for _ in range(WIDE // 128)]
                for j in range(PER_ROW):
                    at = pl.multiple_of((r * PER_ROW + j) * 2 * SUB, 2 * SUB)
                    for a, b, shift, start, stop in pieces(s * POINTS, j * POINTS, POINTS):
                        both = in_ref[pl.ds(at, 2 * SUB), a * 128 : (a + 1) * 128].astype(F32)
                        line[b] = jnp.where((spot >= start) & (spot < stop), move(both, shift), line[b])
                lines.append(jnp.concatenate(line, axis=1))
            for m in range(2):
                joined = jnp.concatenate([line[m * SUB : (m + 1) * SUB] for line in lines], axis=0)
                out_ref[m, r, pair * 2 * SUB : (pair + 1) * 2 * SUB, :] = joined.astype(BF16)[:, :LON]


def call(kernel, out_shape, *operands, **more):
    return pl.pallas_call(
        kernel,
        out_shape=out_shape,
        compiler_params=pltpu.CompilerParams(vmem_limit_bytes=40 * 1024 * 1024),
        **more,
    )(*operands)


def body(
    starting_fields,
    conv_weight,
    norm_gain,
    weight_in,
    weight_out,
    obs_count,
    obs_point,
    obs_channel,
    obs_value,
    obs_precision,
):
    fields = jnp.pad(starting_fields.transpose(0, 2, 1, 3), ((0, 0), (0, 0), (0, 0), (0, WIDE - LON)))
    fields = lax.optimization_barrier(fields)
    bands = lax.axis_size("space")
    odd = lax.axis_index("space") % 2
    top, bottom = fields[:, 0], fields[:, ROWS - 1]
    across = [(i, i + 1 if i % 2 else i - 1) for i in range(1, bands - 1)]
    next_row = lax.ppermute(jnp.where(odd == 1, bottom, top), "space", across)
    within = [(i, i ^ 1) for i in range(bands)]
    chip_row = lax.ppermute(jnp.where(odd == 1, top, bottom), "space", within)
    held = [pltpu.VMEM((2, 2, CHANNELS, WIDE), F32)]
    second = weight_out[0]
    inner, conv, gain, first, observations = call(
        inner_kernel,
        (
            jax.ShapeDtypeStruct((2 * ROW_PACK, PACK), BF16),
            jax.ShapeDtypeStruct((3 * CHANNELS, 3 * CHANNELS), BF16),
            jax.ShapeDtypeStruct((CHANNELS, 128), F32),
            jax.ShapeDtypeStruct((HID, CHANNELS), BF16),
            jax.ShapeDtypeStruct((8, OBS), F32),
        ),
        fields,
        conv_weight,
        norm_gain,
        weight_in[0].T,
        obs_count,
        obs_point[0],
        obs_channel[0],
        obs_value[0],
        obs_precision[0],
        second,
        scratch_shapes=held,
        cost_estimate=pl.CostEstimate(flops=400_000_000, bytes_accessed=2_000_000, transcendentals=500_000),
    )
    weights = (conv, gain, first, second)
    packed = jax.ShapeDtypeStruct((PACK, PACK), BF16)
    sent = call(
        outer_kernel, packed, odd.reshape(1, 1), fields, chip_row, next_row, inner, *weights, scratch_shapes=held
    )

    def exchange(block):
        block = block.reshape(TILES, 2 * SUB, PACK)
        block = lax.all_to_all(block, "member", split_axis=0, concat_axis=0, tiled=True)
        return block.reshape(PACK, PACK)

    tile = exchange(sent)
    own = call(observe_kernel, jax.ShapeDtypeStruct((MEMBERS // 2 + 8, 128), F32), tile, observations)
    around = lax.axis_size("member")
    far = lax.ppermute(own, "member", [(i, (i + 1 if i % 2 else i - 1) % around) for i in range(around)])
    near = lax.ppermute(own, "member", [(i, i ^ 1) for i in range(around)])
    returned = exchange(call(blend_kernel, packed, own, near, far, tile))
    result = call(unpack_kernel, jax.ShapeDtypeStruct((2, ROWS, CHANNELS, LON), BF16), returned)
    return result.transpose(0, 2, 1, 3)


def solution(mesh):
    in_specs = (
        P("member", None, "space", None),
        P(),
        P(),
        P(),
        P(),
        P("space", "member"),
        P("space", "member", None),
        P("space", "member", None),
        P("space", "member", None),
        P("space", "member", None),
    )
    out_specs = P("member", None, "space", None)
    return jax.shard_map(body, mesh=mesh, in_specs=in_specs, out_specs=out_specs, check_vma=False)
```

```python
import jax
import jax.numpy as jnp
from jax import lax
from jax.experimental import pallas as pl
from jax.experimental.pallas import tpu as pltpu
from jax.sharding import PartitionSpec as P

NS_STEPS = 6
NEAR_WEIGHT = 0.5
EPSILON = 1e-06
MEMBERS = 64
CHANNELS = 80
ROWS = 4
LON = 360
WIDE = 384
POINTS = 45
TILES = 32
PER_ROW = 8
SUB = 8
SLOTS = CHANNELS // SUB
PACK = 512
OBS = 256
HID = 320

F32 = jnp.float32
BF16 = jnp.bfloat16


def mm(left, right):
    return jnp.dot(left, right, preferred_element_type=F32)


def mm_t(left, right):
    return lax.dot_general(left, right, (((1,), (1,)), ((), ())), preferred_element_type=F32)


def halves(value):
    high = value.astype(BF16)
    return high, (value - high.astype(F32)).astype(BF16)


def mm_split(left, right, product=mm):
    left_high, left_low = halves(left)
    right_high, right_low = halves(right)
    return product(left_high, right_high) + (
        product(left_high, right_low) + product(left_low, right_high)
    )


def pieces(source, target, length):
    found = []
    done = 0
    while done < length:
        a, b = source + done, target + done
        step = min(length - done, 128 - a % 128, 128 - b % 128)
        found.append((a // 128, b // 128, (b - a) % 128, b % 128, b % 128 + step))
        done += step
    return found


def move(value, shift):
    return pltpu.roll(value, shift, 1) if shift else value


def shift_wrapped(west, here, east, lane):
    end = (LON - 1) % 128
    west_wrap = move(west[:, 256:], 128 - end)
    east_wrap = move(east[:, :128], end)
    west = pltpu.roll(west, 1, 1)
    east = pltpu.roll(east, WIDE - 1, 1)
    west = jnp.concatenate([jnp.where(lane == 0, west_wrap, west[:, :128]), west[:, 128:]], axis=1)
    east = jnp.concatenate([east[:, :256], jnp.where(lane == end, east_wrap, east[:, 256:])], axis=1)
    return here + west + east


def forecast_rows(windows, conv_ref, gain_ref, first_ref, second_ref, held):
    conv = conv_ref[...]
    first = first_ref[...]
    second = second_ref[...]
    gain = gain_ref[:, :1]
    lane = lax.broadcasted_iota(jnp.int32, (CHANNELS, 128), 1)
    for m in range(2):
        near, far = windows[m]
        stacked = jnp.concatenate(
            [jnp.concatenate([near[a], far[a]], axis=1) for a in range(3)], axis=0
        )
        taps = mm(conv, stacked)
        parts = []
        for d, window in enumerate(windows[m]):
            west, here, east = [
                taps[CHANNELS * b : CHANNELS * (b + 1), WIDE * d : WIDE * (d + 1)] for b in range(3)
            ]
            parts.append(window[1].astype(F32) + shift_wrapped(west, here, east, lane))
        updated = jnp.concatenate(parts, axis=1)
        power = jnp.sum(updated * updated, axis=0, keepdims=True) * (1.0 / CHANNELS)
        normed = (updated * lax.rsqrt(power + EPSILON) * gain).astype(BF16)
        hidden = mm(first, normed)
        hidden = (hidden * (0.5 + 0.5 * jnp.tanh(0.5 * hidden))).astype(BF16)
        result = updated + mm(second, hidden)
        held[0, m] = result[:, :WIDE]
        held[1, m] = result[:, WIDE:]


def pack_rows(held, starts, out_ref):
    spot = lax.broadcasted_iota(jnp.int32, (2 * SUB, 128), 1)
    for i, start in enumerate(starts):
        for j in range(PER_ROW):
            packed = [jnp.zeros((2 * SUB, 128), F32) for _ in range(PACK // 128)]
            for s in range(SLOTS):
                for a, b, shift, low, high in pieces(j * POINTS, s * POINTS, POINTS):
                    both = held[i, :, s * SUB : (s + 1) * SUB, a * 128 : (a + 1) * 128]
                    both = move(both.reshape(2 * SUB, 128), shift)
                    packed[b] = jnp.where((spot >= low) & (spot < high), both, packed[b])
            at = start + j * 2 * SUB
            out_ref[at : at + 2 * SUB, :] = jnp.concatenate(packed, axis=1).astype(BF16)


ROW_PACK = PER_ROW * 2 * SUB


def inner_kernel(
    x_ref,
    conv,
    gain,
    first,
    count,
    point,
    channel,
    value,
    precision,
    second_ref,
    out_ref,
    conv_ref,
    gain_ref,
    first_ref,
    obs_ref,
    held,
):
    conv_ref[...] = jnp.concatenate(
        [conv[0, 3 * a : 3 * a + 3].reshape(3 * CHANNELS, CHANNELS) for a in range(3)], axis=1
    )
    row = lax.broadcasted_iota(jnp.int32, (CHANNELS, CHANNELS), 0)
    column = lax.broadcasted_iota(jnp.int32, (CHANNELS, CHANNELS), 1)
    tall = jnp.sum(jnp.where(row == column, gain[...], 0.0), axis=1, keepdims=True)
    gain_ref[...] = jnp.broadcast_to(tall, (CHANNELS, 128))
    first_ref[...] = first[...].astype(F32).T.astype(BF16)
    slots = lax.broadcasted_iota(jnp.int32, (1, OBS), 1)
    obs_ref[0:1, :] = ((channel[...] // SUB) * POINTS + point[...]).astype(F32)
    obs_ref[1:2, :] = (channel[...] % SUB).astype(F32)
    obs_ref[2:3, :] = jnp.where(slots < count[...], precision[...], 0.0)
    obs_ref[3:4, :] = value[...]
    obs_ref[4:, :] = jnp.zeros((4, OBS), F32)
    windows = [[[x_ref[m, r + d] for d in (-1, 0, 1)] for r in (1, 2)] for m in range(2)]
    forecast_rows(windows, conv_ref, gain_ref, first_ref, second_ref, held)
    pack_rows(held, (0, ROW_PACK), out_ref)


def outer_kernel(
    odd_ref,
    x_ref,
    chip_ref,
    next_ref,
    inner_ref,
    conv_ref,
    gain_ref,
    first_ref,
    second_ref,
    out_ref,
    held,
):
    odd = odd_ref[...] == 1
    windows = []
    for m in range(2):
        low = jnp.where(odd, chip_ref[m].astype(F32), next_ref[m].astype(F32)).astype(BF16)
        high = jnp.where(odd, next_ref[m].astype(F32), chip_ref[m].astype(F32)).astype(BF16)
        windows.append([[low, x_ref[m, 0], x_ref[m, 1]], [x_ref[m, 2], x_ref[m, 3], high]])
    forecast_rows(windows, conv_ref, gain_ref, first_ref, second_ref, held)
    pack_rows(held, (0, 3 * ROW_PACK), out_ref)
    out_ref[ROW_PACK : 3 * ROW_PACK, :] = inner_ref[...]


def observe_kernel(tile_ref, obs_ref, out_ref):
    place = lax.broadcasted_iota(jnp.int32, (PACK, OBS), 0)
    lane = obs_ref[0:1, :].astype(jnp.int32)
    sub = obs_ref[1:2, :].astype(jnp.int32)
    weight = obs_ref[2:3, :]
    found = mm(tile_ref[...], jnp.where(place == lane, 1.0, 0.0).astype(BF16))
    found = jnp.where(place % SUB == sub, found, 0.0)
    sampled = jnp.sum(found.reshape(MEMBERS, SUB, OBS), axis=1)
    average = jnp.sum(sampled, axis=0, keepdims=True) * (1.0 / MEMBERS)
    spread = sampled - average
    innovation = obs_ref[3:4, :] - average
    gram = mm_split(spread * weight, spread, mm_t)
    out_ref[: MEMBERS // 2, :MEMBERS] = gram[: MEMBERS // 2]
    out_ref[: MEMBERS // 2, MEMBERS:] = gram[MEMBERS // 2 :]
    pull = jnp.broadcast_to(weight * innovation, (8, OBS))
    out_ref[MEMBERS // 2 :, :MEMBERS] = mm_split(pull, spread, mm_t)
    out_ref[MEMBERS // 2 :, MEMBERS:] = jnp.zeros((8, MEMBERS), F32)


def blend_kernel(own_ref, near_ref, far_ref, tile_ref, out_ref):
    total = own_ref[...] + NEAR_WEIGHT * (near_ref[...] + far_ref[...])
    gram = jnp.concatenate([total[: MEMBERS // 2, :MEMBERS], total[: MEMBERS // 2, MEMBERS:]], axis=0)
    vector = total[MEMBERS // 2 : MEMBERS // 2 + 1, :MEMBERS]
    identity = jnp.where(
        lax.broadcasted_iota(jnp.int32, (MEMBERS, MEMBERS), 0)
        == lax.broadcasted_iota(jnp.int32, (MEMBERS, MEMBERS), 1),
        1.0,
        0.0,
    )
    system = (MEMBERS - 1.0) * identity + gram
    squares = jnp.sum(jnp.sum(system * system, axis=0, keepdims=True), axis=1, keepdims=True)
    scale = jnp.sqrt(squares)
    root = system / scale
    middle = 1.5 * identity - 0.5 * root
    root = mm_split(root, middle)
    inverse = middle
    for sweep in range(1, NS_STEPS):
        middle = 1.5 * identity - 0.5 * mm_split(inverse, root)
        if sweep < NS_STEPS - 1:
            root = mm_split(root, middle)
        inverse = mm_split(middle, inverse)
    once = jnp.sum(inverse * vector, axis=1, keepdims=True)
    mean_weight = jnp.sum(inverse * once, axis=0, keepdims=True) / scale
    full = jnp.sqrt((MEMBERS - 1.0) / scale) * inverse + mean_weight
    mixing = full + (1.0 - jnp.sum(full, axis=1, keepdims=True)) * (1.0 / MEMBERS)
    mixing = mixing.astype(BF16)
    spread_cols = jnp.where(
        lax.broadcasted_iota(jnp.int32, (MEMBERS, PACK), 1) // SUB
        == lax.broadcasted_iota(jnp.int32, (MEMBERS, PACK), 0),
        1.0,
        0.0,
    ).astype(BF16)
    wide = mm(mixing, spread_cols)
    square = jnp.broadcast_to(wide[:, None, :], (MEMBERS, SUB, PACK)).reshape(PACK, PACK)
    same = (
        lax.broadcasted_iota(jnp.int32, (PACK, PACK), 0) % SUB
        == lax.broadcasted_iota(jnp.int32, (PACK, PACK), 1) % SUB
    )
    square = jnp.where(same, square, 0.0).astype(BF16)
    out_ref[...] = mm(square, tile_ref[...]).astype(BF16)


def unpack_kernel(in_ref, out_hbm, laid, sent):
    spot = lax.broadcasted_iota(jnp.int32, (2 * SUB, 128), 1)
    copies = []
    for pair in range(SLOTS // 2):
        rows = []
        for r in range(ROWS):
            lines = []
            for s in (2 * pair, 2 * pair + 1):
                line = [jnp.zeros((2 * SUB, 128), F32) for _ in range(WIDE // 128)]
                for j in range(PER_ROW):
                    at = (r * PER_ROW + j) * 2 * SUB
                    for a, b, shift, low, high in pieces(s * POINTS, j * POINTS, POINTS):
                        both = in_ref[at : at + 2 * SUB, a * 128 : (a + 1) * 128].astype(F32)
                        line[b] = jnp.where((spot >= low) & (spot < high), move(both, shift), line[b])
                lines.append(jnp.concatenate(line, axis=1))
            rows.append(lines)
        block = slice(pair * 2 * SUB, (pair + 1) * 2 * SUB)
        for m in range(2):
            joined = [jnp.concatenate([line[m * SUB : (m + 1) * SUB] for line in lines], axis=0) for lines in rows]
            laid[m, block] = jnp.swapaxes(jnp.stack(joined), 0, 1)[:, :, :LON].astype(BF16)
        copies.append(pltpu.make_async_copy(laid.at[:, block], out_hbm.at[:, block], sent.at[pair]))
        copies[-1].start()
    for copy in copies:
        copy.wait()


def call(kernel, out_shape, *operands, **more):
    return pl.pallas_call(
        kernel,
        out_shape=out_shape,
        compiler_params=pltpu.CompilerParams(vmem_limit_bytes=40 * 1024 * 1024),
        **more,
    )(*operands)


def body(
    starting_fields,
    conv_weight,
    norm_gain,
    weight_in,
    weight_out,
    obs_count,
    obs_point,
    obs_channel,
    obs_value,
    obs_precision,
):
    fields = jnp.pad(starting_fields.transpose(0, 2, 1, 3), ((0, 0), (0, 0), (0, 0), (0, WIDE - LON)))
    fields = lax.optimization_barrier(fields)
    bands = lax.axis_size("space")
    odd = lax.axis_index("space") % 2
    top, bottom = fields[:, 0], fields[:, ROWS - 1]
    across = [(i, i + 1 if i % 2 else i - 1) for i in range(1, bands - 1)]
    next_row = lax.ppermute(jnp.where(odd == 1, bottom, top), "space", across)
    within = [(i, i ^ 1) for i in range(bands)]
    chip_row = lax.ppermute(jnp.where(odd == 1, top, bottom), "space", within)
    held = [pltpu.VMEM((2, 2, CHANNELS, WIDE), F32)]
    second = weight_out[0]
    inner, conv, gain, first, observations = call(
        inner_kernel,
        (
            jax.ShapeDtypeStruct((2 * ROW_PACK, PACK), BF16),
            jax.ShapeDtypeStruct((3 * CHANNELS, 3 * CHANNELS), BF16),
            jax.ShapeDtypeStruct((CHANNELS, 128), F32),
            jax.ShapeDtypeStruct((HID, CHANNELS), BF16),
            jax.ShapeDtypeStruct((8, OBS), F32),
        ),
        fields,
        conv_weight,
        norm_gain,
        weight_in[0].T,
        obs_count,
        obs_point[0],
        obs_channel[0],
        obs_value[0],
        obs_precision[0],
        second,
        scratch_shapes=held,
        cost_estimate=pl.CostEstimate(flops=400_000_000, bytes_accessed=2_000_000, transcendentals=500_000),
    )
    weights = (conv, gain, first, second)
    packed = jax.ShapeDtypeStruct((PACK, PACK), BF16)
    sent = call(
        outer_kernel, packed, odd.reshape(1, 1), fields, chip_row, next_row, inner, *weights, scratch_shapes=held
    )

    def exchange(block):
        block = block.reshape(TILES, 2 * SUB, PACK)
        block = lax.all_to_all(block, "member", split_axis=0, concat_axis=0, tiled=True)
        return block.reshape(PACK, PACK)

    tile = exchange(sent)
    own = call(observe_kernel, jax.ShapeDtypeStruct((MEMBERS // 2 + 8, 128), F32), tile, observations)
    around = lax.axis_size("member")
    far = lax.ppermute(own, "member", [(i, (i + 1 if i % 2 else i - 1) % around) for i in range(around)])
    near = lax.ppermute(own, "member", [(i, i ^ 1) for i in range(around)])
    returned = exchange(call(blend_kernel, packed, own, near, far, tile))
    return call(
        unpack_kernel,
        jax.ShapeDtypeStruct((2, CHANNELS, ROWS, LON), BF16),
        returned,
        out_specs=pl.BlockSpec(memory_space=pl.ANY),
        scratch_shapes=[pltpu.VMEM((2, CHANNELS, ROWS, LON), BF16), pltpu.SemaphoreType.DMA((SLOTS // 2,))],
    )


def solution(mesh):
    in_specs = (
        P("member", None, "space", None),
        P(),
        P(),
        P(),
        P(),
        P("space", "member"),
        P("space", "member", None),
        P("space", "member", None),
        P("space", "member", None),
        P("space", "member", None),
    )
    out_specs = P("member", None, "space", None)
    return jax.shard_map(body, mesh=mesh, in_specs=in_specs, out_specs=out_specs, check_vma=False)
```

```python
import jax
import jax.numpy as jnp
from jax import lax
from jax.experimental import pallas as pl
from jax.experimental.pallas import tpu as pltpu
from jax.sharding import PartitionSpec as P

NS_STEPS = 6
NEAR_WEIGHT = 0.5
EPSILON = 1e-06
MEMBERS = 64
CHANNELS = 80
ROWS = 4
LON = 360
WIDE = 384
POINTS = 45
TILES = 32
BANDS = 8
PER_ROW = 8
SUB = 8
SLOTS = CHANNELS // SUB
PACK = 512
OBS = 256
HID = 320

F32 = jnp.float32
BF16 = jnp.bfloat16


def mm(left, right):
    return jnp.dot(left, right, preferred_element_type=F32)


def mm_t(left, right):
    return lax.dot_general(left, right, (((1,), (1,)), ((), ())), preferred_element_type=F32)


def halves(value):
    high = value.astype(BF16)
    return high, (value - high.astype(F32)).astype(BF16)


def mm_split(left, right, product=mm):
    left_high, left_low = halves(left)
    right_high, right_low = halves(right)
    return product(left_high, right_high) + (
        product(left_high, right_low) + product(left_low, right_high)
    )


def pieces(source, target, length):
    found = []
    done = 0
    while done < length:
        a, b = source + done, target + done
        step = min(length - done, 128 - a % 128, 128 - b % 128)
        found.append((a // 128, b // 128, (b - a) % 128, b % 128, b % 128 + step))
        done += step
    return found


def move(value, shift):
    return pltpu.roll(value, shift, 1) if shift else value


def shift_wrapped(west, here, east, lane):
    end = (LON - 1) % 128
    west_wrap = move(west[:, 256:], 128 - end)
    east_wrap = move(east[:, :128], end)
    west = pltpu.roll(west, 1, 1)
    east = pltpu.roll(east, WIDE - 1, 1)
    west = jnp.concatenate([jnp.where(lane == 0, west_wrap, west[:, :128]), west[:, 128:]], axis=1)
    east = jnp.concatenate([east[:, :256], jnp.where(lane == end, east_wrap, east[:, 256:])], axis=1)
    return here + west + east


def convolve(windows, conv):
    lane = lax.broadcasted_iota(jnp.int32, (CHANNELS, 128), 1)
    near, far = windows
    stacked = jnp.concatenate([jnp.concatenate([near[a], far[a]], axis=1) for a in range(3)], axis=0)
    taps = mm(conv, stacked)
    parts = []
    for d, window in enumerate(windows):
        west, here, east = [
            taps[CHANNELS * b : CHANNELS * (b + 1), WIDE * d : WIDE * (d + 1)] for b in range(3)
        ]
        parts.append(window[1].astype(F32) + shift_wrapped(west, here, east, lane))
    return jnp.concatenate(parts, axis=1)


def pointwise(updated, gain, first, second, held, m):
    power = jnp.sum(updated * updated, axis=0, keepdims=True) * (1.0 / CHANNELS)
    normed = (updated * lax.rsqrt(power + EPSILON) * gain).astype(BF16)
    hidden = mm(first, normed)
    hidden = (hidden * (0.5 + 0.5 * jnp.tanh(0.5 * hidden))).astype(BF16)
    result = updated + mm(second, hidden)
    held[0, m] = result[:, :WIDE]
    held[1, m] = result[:, WIDE:]


def pack_rows(held, starts, out_ref):
    spot = lax.broadcasted_iota(jnp.int32, (2 * SUB, 128), 1)
    for i, start in enumerate(starts):
        for j in range(PER_ROW):
            packed = [jnp.zeros((2 * SUB, 128), F32) for _ in range(PACK // 128)]
            for s in range(SLOTS):
                for a, b, shift, low, high in pieces(j * POINTS, s * POINTS, POINTS):
                    both = held[i, :, s * SUB : (s + 1) * SUB, a * 128 : (a + 1) * 128]
                    both = move(both.reshape(2 * SUB, 128), shift)
                    packed[b] = jnp.where((spot >= low) & (spot < high), both, packed[b])
            at = start + j * 2 * SUB
            out_ref[at : at + 2 * SUB, :] = jnp.concatenate(packed, axis=1).astype(BF16)


ROW_PACK = PER_ROW * 2 * SUB


def inner_kernel(
    x_ref,
    conv,
    first,
    second_ref,
    count,
    gain_hbm,
    point_hbm,
    channel_hbm,
    value_hbm,
    precision_hbm,
    out_ref,
    conv_ref,
    gain_ref,
    first_ref,
    obs_ref,
    held,
    updated,
    gain,
    point,
    channel,
    value,
    precision,
    arrived,
):
    moves = [(gain_hbm, gain), (point_hbm, point), (channel_hbm, channel)]
    moves += [(value_hbm, value), (precision_hbm, precision)]
    copies = [pltpu.make_async_copy(source, target, arrived.at[i]) for i, (source, target) in enumerate(moves)]
    for copy in copies:
        copy.start()
    conv_ref[...] = jnp.concatenate(
        [conv[0, 3 * a : 3 * a + 3].reshape(3 * CHANNELS, CHANNELS) for a in range(3)], axis=1
    )
    first_ref[...] = first[...].astype(F32).T.astype(BF16)
    for m in range(2):
        updated[m] = convolve([[x_ref[m, r + d] for d in (-1, 0, 1)] for r in (1, 2)], conv_ref[...])
    copies[0].wait()
    row = lax.broadcasted_iota(jnp.int32, (CHANNELS, CHANNELS), 0)
    column = lax.broadcasted_iota(jnp.int32, (CHANNELS, CHANNELS), 1)
    tall = jnp.sum(jnp.where(row == column, gain[...], 0.0), axis=1, keepdims=True)
    gain_ref[...] = jnp.broadcast_to(tall, (CHANNELS, 128))
    for m in range(2):
        pointwise(updated[m], gain_ref[:, :1], first_ref[...], second_ref[...], held, m)
    pack_rows(held, (0, ROW_PACK), out_ref)
    for copy in copies[1:]:
        copy.wait()
    slots = lax.broadcasted_iota(jnp.int32, (1, OBS), 1)
    obs_ref[0:1, :] = ((channel[...] // SUB) * POINTS + point[...]).astype(F32)
    obs_ref[1:2, :] = (channel[...] % SUB).astype(F32)
    obs_ref[2:3, :] = jnp.where(slots < count[...], precision[...], 0.0)
    obs_ref[3:4, :] = value[...]
    obs_ref[4:, :] = jnp.zeros((4, OBS), F32)


def outer_kernel(
    band_ref,
    x_ref,
    chip_ref,
    next_ref,
    inner_ref,
    conv_ref,
    gain_ref,
    first_ref,
    second_ref,
    out_ref,
    held,
):
    band = band_ref[...]
    odd = band % 2 == 1
    windows = []
    for m in range(2):
        chip = chip_ref[m].astype(F32)
        beyond = next_ref[m].astype(F32)
        low = jnp.where(band == 0, 0.0, jnp.where(odd, chip, beyond)).astype(BF16)
        high = jnp.where(band == BANDS - 1, 0.0, jnp.where(odd, beyond, chip)).astype(BF16)
        windows.append([[low, x_ref[m, 0], x_ref[m, 1]], [x_ref[m, 2], x_ref[m, 3], high]])
    for m in range(2):
        updated = convolve(windows[m], conv_ref[...])
        pointwise(updated, gain_ref[:, :1], first_ref[...], second_ref[...], held, m)
    pack_rows(held, (0, 3 * ROW_PACK), out_ref)
    out_ref[ROW_PACK : 3 * ROW_PACK, :] = inner_ref[...]


def observe_kernel(tile_ref, obs_ref, out_ref):
    place = lax.broadcasted_iota(jnp.int32, (PACK, OBS), 0)
    lane = obs_ref[0:1, :].astype(jnp.int32)
    sub = obs_ref[1:2, :].astype(jnp.int32)
    weight = obs_ref[2:3, :]
    found = mm(tile_ref[...], jnp.where(place == lane, 1.0, 0.0).astype(BF16))
    found = jnp.where(place % SUB == sub, found, 0.0)
    sampled = jnp.sum(found.reshape(MEMBERS, SUB, OBS), axis=1)
    average = jnp.sum(sampled, axis=0, keepdims=True) * (1.0 / MEMBERS)
    spread = sampled - average
    innovation = obs_ref[3:4, :] - average
    gram = mm_split(spread * weight, spread, mm_t)
    out_ref[: MEMBERS // 2, :MEMBERS] = gram[: MEMBERS // 2]
    out_ref[: MEMBERS // 2, MEMBERS:] = gram[MEMBERS // 2 :]
    pull = jnp.broadcast_to(weight * innovation, (8, OBS))
    out_ref[MEMBERS // 2 :, :MEMBERS] = mm_split(pull, spread, mm_t)
    out_ref[MEMBERS // 2 :, MEMBERS:] = jnp.zeros((8, MEMBERS), F32)


def blend_kernel(own_ref, near_ref, far_ref, tile_ref, out_ref):
    total = own_ref[...] + NEAR_WEIGHT * (near_ref[...] + far_ref[...])
    gram = jnp.concatenate([total[: MEMBERS // 2, :MEMBERS], total[: MEMBERS // 2, MEMBERS:]], axis=0)
    vector = total[MEMBERS // 2 : MEMBERS // 2 + 1, :MEMBERS]
    identity = jnp.where(
        lax.broadcasted_iota(jnp.int32, (MEMBERS, MEMBERS), 0)
        == lax.broadcasted_iota(jnp.int32, (MEMBERS, MEMBERS), 1),
        1.0,
        0.0,
    )
    system = (MEMBERS - 1.0) * identity + gram
    squares = jnp.sum(jnp.sum(system * system, axis=0, keepdims=True), axis=1, keepdims=True)
    scale = jnp.sqrt(squares)
    root = system / scale
    middle = 1.5 * identity - 0.5 * root
    root = mm_split(root, middle)
    inverse = middle
    for sweep in range(1, NS_STEPS):
        middle = 1.5 * identity - 0.5 * mm_split(inverse, root)
        if sweep < NS_STEPS - 1:
            root = mm_split(root, middle)
        inverse = mm_split(middle, inverse)
    once = jnp.sum(inverse * vector, axis=1, keepdims=True)
    mean_weight = jnp.sum(inverse * once, axis=0, keepdims=True) / scale
    full = jnp.sqrt((MEMBERS - 1.0) / scale) * inverse + mean_weight
    mixing = full + (1.0 - jnp.sum(full, axis=1, keepdims=True)) * (1.0 / MEMBERS)
    mixing = mixing.astype(BF16)
    spread_cols = jnp.where(
        lax.broadcasted_iota(jnp.int32, (MEMBERS, PACK), 1) // SUB
        == lax.broadcasted_iota(jnp.int32, (MEMBERS, PACK), 0),
        1.0,
        0.0,
    ).astype(BF16)
    wide = mm(mixing, spread_cols)
    square = jnp.broadcast_to(wide[:, None, :], (MEMBERS, SUB, PACK)).reshape(PACK, PACK)
    same = (
        lax.broadcasted_iota(jnp.int32, (PACK, PACK), 0) % SUB
        == lax.broadcasted_iota(jnp.int32, (PACK, PACK), 1) % SUB
    )
    square = jnp.where(same, square, 0.0).astype(BF16)
    out_ref[...] = mm(square, tile_ref[...]).astype(BF16)


def unpack_kernel(in_ref, out_hbm, laid, sent):
    spot = lax.broadcasted_iota(jnp.int32, (2 * SUB, 128), 1)
    copies = []
    for pair in range(SLOTS // 2):
        rows = []
        for r in range(ROWS):
            lines = []
            for s in (2 * pair, 2 * pair + 1):
                line = [jnp.zeros((2 * SUB, 128), F32) for _ in range(WIDE // 128)]
                for j in range(PER_ROW):
                    at = (r * PER_ROW + j) * 2 * SUB
                    for a, b, shift, low, high in pieces(s * POINTS, j * POINTS, POINTS):
                        both = in_ref[at : at + 2 * SUB, a * 128 : (a + 1) * 128].astype(F32)
                        line[b] = jnp.where((spot >= low) & (spot < high), move(both, shift), line[b])
                lines.append(jnp.concatenate(line, axis=1))
            rows.append(lines)
        block = slice(pair * 2 * SUB, (pair + 1) * 2 * SUB)
        for m in range(2):
            joined = [jnp.concatenate([line[m * SUB : (m + 1) * SUB] for line in lines], axis=0) for lines in rows]
            laid[m, block] = jnp.swapaxes(jnp.stack(joined), 0, 1)[:, :, :LON].astype(BF16)
        copies.append(pltpu.make_async_copy(laid.at[:, block], out_hbm.at[:, block], sent.at[pair]))
        copies[-1].start()
    for copy in copies:
        copy.wait()


def call(kernel, out_shape, *operands, **more):
    return pl.pallas_call(
        kernel,
        out_shape=out_shape,
        compiler_params=pltpu.CompilerParams(vmem_limit_bytes=40 * 1024 * 1024),
        **more,
    )(*operands)


def body(
    starting_fields,
    conv_weight,
    norm_gain,
    weight_in,
    weight_out,
    obs_count,
    obs_point,
    obs_channel,
    obs_value,
    obs_precision,
):
    fields = jnp.pad(starting_fields.transpose(0, 2, 1, 3), ((0, 0), (0, 0), (0, 0), (0, WIDE - LON)))
    fields = lax.optimization_barrier(fields)
    band = lax.axis_index("space")
    odd = band % 2
    top, bottom = fields[:, 0], fields[:, ROWS - 1]
    across = [(i, (i + 1 if i % 2 else i - 1) % BANDS) for i in range(BANDS)]
    next_row = lax.ppermute(jnp.where(odd == 1, bottom, top), "space", across)
    within = [(i, i ^ 1) for i in range(BANDS)]
    chip_row = lax.ppermute(jnp.where(odd == 1, top, bottom), "space", within)
    held = [pltpu.VMEM((2, 2, CHANNELS, WIDE), F32)]
    second = weight_out[0]
    small = [
        (norm_gain, F32, (1, CHANNELS)),
        (obs_point[0], jnp.int32, (1, OBS)),
        (obs_channel[0], jnp.int32, (1, OBS)),
        (obs_value[0], F32, (1, OBS)),
        (obs_precision[0], F32, (1, OBS)),
    ]
    inner, conv, gain, first, observations = call(
        inner_kernel,
        (
            jax.ShapeDtypeStruct((2 * ROW_PACK, PACK), BF16),
            jax.ShapeDtypeStruct((3 * CHANNELS, 3 * CHANNELS), BF16),
            jax.ShapeDtypeStruct((CHANNELS, 128), F32),
            jax.ShapeDtypeStruct((HID, CHANNELS), BF16),
            jax.ShapeDtypeStruct((8, OBS), F32),
        ),
        fields,
        conv_weight,
        weight_in[0].T,
        second,
        obs_count,
        *[pltpu.with_memory_space_constraint(array, pltpu.HBM) for array, _, _ in small],
        in_specs=[pl.BlockSpec(memory_space=pltpu.VMEM)] * 5 + [pl.BlockSpec(memory_space=pltpu.HBM)] * 5,
        scratch_shapes=held
        + [pltpu.VMEM((2, CHANNELS, 2 * WIDE), F32)]
        + [pltpu.VMEM(shape, kind) for _, kind, shape in small]
        + [pltpu.SemaphoreType.DMA((len(small),))],
        cost_estimate=pl.CostEstimate(flops=400_000_000, bytes_accessed=2_000_000, transcendentals=500_000),
    )
    weights = (conv, gain, first, second)
    packed = jax.ShapeDtypeStruct((PACK, PACK), BF16)
    sent = call(
        outer_kernel, packed, band.reshape(1, 1), fields, chip_row, next_row, inner, *weights, scratch_shapes=held
    )

    def exchange(block):
        block = block.reshape(TILES, 2 * SUB, PACK)
        block = lax.all_to_all(block, "member", split_axis=0, concat_axis=0, tiled=True)
        return block.reshape(PACK, PACK)

    tile = exchange(sent)
    own = call(observe_kernel, jax.ShapeDtypeStruct((MEMBERS // 2 + 8, 128), F32), tile, observations)
    around = lax.axis_size("member")
    far = lax.ppermute(own, "member", [(i, (i + 1 if i % 2 else i - 1) % around) for i in range(around)])
    near = lax.ppermute(own, "member", [(i, i ^ 1) for i in range(around)])
    returned = exchange(call(blend_kernel, packed, own, near, far, tile))
    return call(
        unpack_kernel,
        jax.ShapeDtypeStruct((2, CHANNELS, ROWS, LON), BF16),
        returned,
        out_specs=pl.BlockSpec(memory_space=pl.ANY),
        scratch_shapes=[pltpu.VMEM((2, CHANNELS, ROWS, LON), BF16), pltpu.SemaphoreType.DMA((SLOTS // 2,))],
    )


def solution(mesh):
    in_specs = (
        P("member", None, "space", None),
        P(),
        P(),
        P(),
        P(),
        P("space", "member"),
        P("space", "member", None),
        P("space", "member", None),
        P("space", "member", None),
        P("space", "member", None),
    )
    out_specs = P("member", None, "space", None)
    return jax.shard_map(body, mesh=mesh, in_specs=in_specs, out_specs=out_specs, check_vma=False)
```

```python
import jax
import jax.numpy as jnp
from jax import lax
from jax.experimental import pallas as pl
from jax.experimental.pallas import tpu as pltpu
from jax.sharding import PartitionSpec as P

NS_STEPS = 6
NEAR_WEIGHT = 0.5
EPSILON = 1e-06
MEMBERS = 64
CHANNELS = 80
ROWS = 4
LON = 360
WIDE = 384
POINTS = 45
TILES = 32
BANDS = 8
PER_ROW = 8
SUB = 8
SLOTS = CHANNELS // SUB
PACK = 512
OBS = 256
HID = 320

F32 = jnp.float32
BF16 = jnp.bfloat16


def mm(left, right):
    return jnp.dot(left, right, preferred_element_type=F32)


def mm_t(left, right):
    return lax.dot_general(left, right, (((1,), (1,)), ((), ())), preferred_element_type=F32)


def halves(value):
    high = value.astype(BF16)
    return high, (value - high.astype(F32)).astype(BF16)


def mm_split(left, right, product=mm):
    left_high, left_low = halves(left)
    right_high, right_low = halves(right)
    return product(left_high, right_high) + (
        product(left_high, right_low) + product(left_low, right_high)
    )


def pieces(source, target, length):
    found = []
    done = 0
    while done < length:
        a, b = source + done, target + done
        step = min(length - done, 128 - a % 128, 128 - b % 128)
        found.append((a // 128, b // 128, (b - a) % 128, b % 128, b % 128 + step))
        done += step
    return found


def move(value, shift):
    return pltpu.roll(value, shift, 1) if shift else value


def shift_wrapped(west, here, east, lane):
    end = (LON - 1) % 128
    west_wrap = move(west[:, 256:], 128 - end)
    east_wrap = move(east[:, :128], end)
    west = pltpu.roll(west, 1, 1)
    east = pltpu.roll(east, WIDE - 1, 1)
    west = jnp.concatenate([jnp.where(lane == 0, west_wrap, west[:, :128]), west[:, 128:]], axis=1)
    east = jnp.concatenate([east[:, :256], jnp.where(lane == end, east_wrap, east[:, 256:])], axis=1)
    return here + west + east


def forecast_rows(windows, conv_ref, gain_ref, first_ref, second_ref, held, ready=None):
    conv = conv_ref[...]
    first = first_ref[...]
    second = second_ref[...]
    lane = lax.broadcasted_iota(jnp.int32, (CHANNELS, 128), 1)
    for m in range(2):
        near, far = windows[m]
        stacked = jnp.concatenate(
            [jnp.concatenate([near[a], far[a]], axis=1) for a in range(3)], axis=0
        )
        taps = mm(conv, stacked)
        parts = []
        for d, window in enumerate(windows[m]):
            west, here, east = [
                taps[CHANNELS * b : CHANNELS * (b + 1), WIDE * d : WIDE * (d + 1)] for b in range(3)
            ]
            parts.append(window[1].astype(F32) + shift_wrapped(west, here, east, lane))
        updated = jnp.concatenate(parts, axis=1)
        if ready is not None and m == 0:
            ready()
        gain = gain_ref[:, :1]
        power = jnp.sum(updated * updated, axis=0, keepdims=True) * (1.0 / CHANNELS)
        normed = (updated * lax.rsqrt(power + EPSILON) * gain).astype(BF16)
        hidden = mm(first, normed)
        hidden = (hidden * (0.5 + 0.5 * jnp.tanh(0.5 * hidden))).astype(BF16)
        result = updated + mm(second, hidden)
        held[0, m] = result[:, :WIDE]
        held[1, m] = result[:, WIDE:]


def pack_rows(held, starts, out_ref):
    spot = lax.broadcasted_iota(jnp.int32, (2 * SUB, 128), 1)
    for i, start in enumerate(starts):
        for j in range(PER_ROW):
            packed = [jnp.zeros((2 * SUB, 128), F32) for _ in range(PACK // 128)]
            for s in range(SLOTS):
                for a, b, shift, low, high in pieces(j * POINTS, s * POINTS, POINTS):
                    both = held[i, :, s * SUB : (s + 1) * SUB, a * 128 : (a + 1) * 128]
                    both = move(both.reshape(2 * SUB, 128), shift)
                    packed[b] = jnp.where((spot >= low) & (spot < high), both, packed[b])
            at = start + j * 2 * SUB
            out_ref[at : at + 2 * SUB, :] = jnp.concatenate(packed, axis=1).astype(BF16)


ROW_PACK = PER_ROW * 2 * SUB


def inner_kernel(
    x_ref,
    conv,
    first,
    second_ref,
    count,
    gain_hbm,
    point_hbm,
    channel_hbm,
    value_hbm,
    precision_hbm,
    out_ref,
    conv_ref,
    gain_ref,
    first_ref,
    obs_ref,
    held,
    gain,
    point,
    channel,
    value,
    precision,
    arrived,
):
    moves = [(gain_hbm, gain), (point_hbm, point), (channel_hbm, channel)]
    moves += [(value_hbm, value), (precision_hbm, precision)]
    copies = [pltpu.make_async_copy(source, target, arrived.at[i]) for i, (source, target) in enumerate(moves)]
    for copy in copies:
        copy.start()
    conv_ref[...] = jnp.concatenate(
        [conv[0, 3 * a : 3 * a + 3].reshape(3 * CHANNELS, CHANNELS) for a in range(3)], axis=1
    )
    first_ref[...] = first[...].astype(F32).T.astype(BF16)

    def ready():
        for copy in copies:
            copy.wait()
        row = lax.broadcasted_iota(jnp.int32, (CHANNELS, CHANNELS), 0)
        column = lax.broadcasted_iota(jnp.int32, (CHANNELS, CHANNELS), 1)
        tall = jnp.sum(jnp.where(row == column, gain[...], 0.0), axis=1, keepdims=True)
        gain_ref[...] = jnp.broadcast_to(tall, (CHANNELS, 128))
        slots = lax.broadcasted_iota(jnp.int32, (1, OBS), 1)
        obs_ref[0:1, :] = ((channel[...] // SUB) * POINTS + point[...]).astype(F32)
        obs_ref[1:2, :] = (channel[...] % SUB).astype(F32)
        obs_ref[2:3, :] = jnp.where(slots < count[...], precision[...], 0.0)
        obs_ref[3:4, :] = value[...]
        obs_ref[4:, :] = jnp.zeros((4, OBS), F32)

    windows = [[[x_ref[m, r + d] for d in (-1, 0, 1)] for r in (1, 2)] for m in range(2)]
    forecast_rows(windows, conv_ref, gain_ref, first_ref, second_ref, held, ready)
    pack_rows(held, (0, ROW_PACK), out_ref)


def outer_kernel(
    band_ref,
    x_ref,
    chip_ref,
    next_ref,
    inner_ref,
    conv_ref,
    gain_ref,
    first_ref,
    second_ref,
    out_ref,
    held,
):
    band = band_ref[...]
    odd = band % 2 == 1
    windows = []
    for m in range(2):
        chip = chip_ref[m].astype(F32)
        beyond = next_ref[m].astype(F32)
        low = jnp.where(band == 0, 0.0, jnp.where(odd, chip, beyond)).astype(BF16)
        high = jnp.where(band == BANDS - 1, 0.0, jnp.where(odd, beyond, chip)).astype(BF16)
        windows.append([[low, x_ref[m, 0], x_ref[m, 1]], [x_ref[m, 2], x_ref[m, 3], high]])
    forecast_rows(windows, conv_ref, gain_ref, first_ref, second_ref, held)
    pack_rows(held, (0, 3 * ROW_PACK), out_ref)
    out_ref[ROW_PACK : 3 * ROW_PACK, :] = inner_ref[...]


def observe_kernel(tile_ref, obs_ref, out_ref):
    place = lax.broadcasted_iota(jnp.int32, (PACK, OBS), 0)
    lane = obs_ref[0:1, :].astype(jnp.int32)
    sub = obs_ref[1:2, :].astype(jnp.int32)
    weight = obs_ref[2:3, :]
    found = mm(tile_ref[...], jnp.where(place == lane, 1.0, 0.0).astype(BF16))
    found = jnp.where(place % SUB == sub, found, 0.0)
    sampled = jnp.sum(found.reshape(MEMBERS, SUB, OBS), axis=1)
    average = jnp.sum(sampled, axis=0, keepdims=True) * (1.0 / MEMBERS)
    spread = sampled - average
    innovation = obs_ref[3:4, :] - average
    gram = mm_split(spread * weight, spread, mm_t)
    out_ref[: MEMBERS // 2, :MEMBERS] = gram[: MEMBERS // 2]
    out_ref[: MEMBERS // 2, MEMBERS:] = gram[MEMBERS // 2 :]
    pull = jnp.broadcast_to(weight * innovation, (8, OBS))
    out_ref[MEMBERS // 2 :, :MEMBERS] = mm_split(pull, spread, mm_t)
    out_ref[MEMBERS // 2 :, MEMBERS:] = jnp.zeros((8, MEMBERS), F32)


def blend_kernel(own_ref, near_ref, far_ref, tile_ref, out_ref):
    total = own_ref[...] + NEAR_WEIGHT * (near_ref[...] + far_ref[...])
    gram = jnp.concatenate([total[: MEMBERS // 2, :MEMBERS], total[: MEMBERS // 2, MEMBERS:]], axis=0)
    vector = total[MEMBERS // 2 : MEMBERS // 2 + 1, :MEMBERS]
    identity = jnp.where(
        lax.broadcasted_iota(jnp.int32, (MEMBERS, MEMBERS), 0)
        == lax.broadcasted_iota(jnp.int32, (MEMBERS, MEMBERS), 1),
        1.0,
        0.0,
    )
    system = (MEMBERS - 1.0) * identity + gram
    squares = jnp.sum(jnp.sum(system * system, axis=0, keepdims=True), axis=1, keepdims=True)
    scale = jnp.sqrt(squares)
    root = system / scale
    middle = 1.5 * identity - 0.5 * root
    root = mm_split(root, middle)
    inverse = middle
    for sweep in range(1, NS_STEPS):
        middle = 1.5 * identity - 0.5 * mm_split(inverse, root)
        if sweep < NS_STEPS - 1:
            root = mm_split(root, middle)
        inverse = mm_split(middle, inverse)
    once = jnp.sum(inverse * vector, axis=1, keepdims=True)
    mean_weight = jnp.sum(inverse * once, axis=0, keepdims=True) / scale
    full = jnp.sqrt((MEMBERS - 1.0) / scale) * inverse + mean_weight
    mixing = full + (1.0 - jnp.sum(full, axis=1, keepdims=True)) * (1.0 / MEMBERS)
    mixing = mixing.astype(BF16)
    spread_cols = jnp.where(
        lax.broadcasted_iota(jnp.int32, (MEMBERS, PACK), 1) // SUB
        == lax.broadcasted_iota(jnp.int32, (MEMBERS, PACK), 0),
        1.0,
        0.0,
    ).astype(BF16)
    wide = mm(mixing, spread_cols)
    square = jnp.broadcast_to(wide[:, None, :], (MEMBERS, SUB, PACK)).reshape(PACK, PACK)
    same = (
        lax.broadcasted_iota(jnp.int32, (PACK, PACK), 0) % SUB
        == lax.broadcasted_iota(jnp.int32, (PACK, PACK), 1) % SUB
    )
    square = jnp.where(same, square, 0.0).astype(BF16)
    out_ref[...] = mm(square, tile_ref[...]).astype(BF16)


def unpack_kernel(in_ref, out_hbm, laid, sent):
    spot = lax.broadcasted_iota(jnp.int32, (2 * SUB, 128), 1)
    copies = []
    for pair in range(SLOTS // 2):
        rows = []
        for r in range(ROWS):
            lines = []
            for s in (2 * pair, 2 * pair + 1):
                line = [jnp.zeros((2 * SUB, 128), F32) for _ in range(WIDE // 128)]
                for j in range(PER_ROW):
                    at = (r * PER_ROW + j) * 2 * SUB
                    for a, b, shift, low, high in pieces(s * POINTS, j * POINTS, POINTS):
                        both = in_ref[at : at + 2 * SUB, a * 128 : (a + 1) * 128].astype(F32)
                        line[b] = jnp.where((spot >= low) & (spot < high), move(both, shift), line[b])
                lines.append(jnp.concatenate(line, axis=1))
            rows.append(lines)
        block = slice(pair * 2 * SUB, (pair + 1) * 2 * SUB)
        for m in range(2):
            joined = [jnp.concatenate([line[m * SUB : (m + 1) * SUB] for line in lines], axis=0) for lines in rows]
            laid[m, block] = jnp.swapaxes(jnp.stack(joined), 0, 1)[:, :, :LON].astype(BF16)
        copies.append(pltpu.make_async_copy(laid.at[:, block], out_hbm.at[:, block], sent.at[pair]))
        copies[-1].start()
    for copy in copies:
        copy.wait()


def call(kernel, out_shape, *operands, **more):
    return pl.pallas_call(
        kernel,
        out_shape=out_shape,
        compiler_params=pltpu.CompilerParams(vmem_limit_bytes=40 * 1024 * 1024),
        **more,
    )(*operands)


def body(
    starting_fields,
    conv_weight,
    norm_gain,
    weight_in,
    weight_out,
    obs_count,
    obs_point,
    obs_channel,
    obs_value,
    obs_precision,
):
    fields = jnp.pad(starting_fields.transpose(0, 2, 1, 3), ((0, 0), (0, 0), (0, 0), (0, WIDE - LON)))
    fields = lax.optimization_barrier(fields)
    band = lax.axis_index("space")
    odd = band % 2
    top, bottom = fields[:, 0], fields[:, ROWS - 1]
    across = [(i, (i + 1 if i % 2 else i - 1) % BANDS) for i in range(BANDS)]
    next_row = lax.ppermute(jnp.where(odd == 1, bottom, top), "space", across)
    within = [(i, i ^ 1) for i in range(BANDS)]
    chip_row = lax.ppermute(jnp.where(odd == 1, top, bottom), "space", within)
    held = [pltpu.VMEM((2, 2, CHANNELS, WIDE), F32)]
    second = weight_out[0]
    small = [
        (norm_gain, F32, (1, CHANNELS)),
        (obs_point[0], jnp.int32, (1, OBS)),
        (obs_channel[0], jnp.int32, (1, OBS)),
        (obs_value[0], F32, (1, OBS)),
        (obs_precision[0], F32, (1, OBS)),
    ]
    inner, conv, gain, first, observations = call(
        inner_kernel,
        (
            jax.ShapeDtypeStruct((2 * ROW_PACK, PACK), BF16),
            jax.ShapeDtypeStruct((3 * CHANNELS, 3 * CHANNELS), BF16),
            jax.ShapeDtypeStruct((CHANNELS, 128), F32),
            jax.ShapeDtypeStruct((HID, CHANNELS), BF16),
            jax.ShapeDtypeStruct((8, OBS), F32),
        ),
        fields,
        conv_weight,
        weight_in[0].T,
        second,
        obs_count,
        *[pltpu.with_memory_space_constraint(array, pltpu.HBM) for array, _, _ in small],
        in_specs=[pl.BlockSpec(memory_space=pltpu.VMEM)] * 5 + [pl.BlockSpec(memory_space=pltpu.HBM)] * 5,
        scratch_shapes=held
        + [pltpu.VMEM(shape, kind) for _, kind, shape in small]
        + [pltpu.SemaphoreType.DMA((len(small),))],
        cost_estimate=pl.CostEstimate(flops=400_000_000, bytes_accessed=2_000_000, transcendentals=500_000),
    )
    weights = (conv, gain, first, second)
    packed = jax.ShapeDtypeStruct((PACK, PACK), BF16)
    sent = call(
        outer_kernel, packed, band.reshape(1, 1), fields, chip_row, next_row, inner, *weights, scratch_shapes=held
    )

    def exchange(block):
        block = block.reshape(TILES, 2 * SUB, PACK)
        block = lax.all_to_all(block, "member", split_axis=0, concat_axis=0, tiled=True)
        return block.reshape(PACK, PACK)

    tile = exchange(sent)
    own = call(observe_kernel, jax.ShapeDtypeStruct((MEMBERS // 2 + 8, 128), F32), tile, observations)
    around = lax.axis_size("member")
    far = lax.ppermute(own, "member", [(i, (i + 1 if i % 2 else i - 1) % around) for i in range(around)])
    near = lax.ppermute(own, "member", [(i, i ^ 1) for i in range(around)])
    returned = exchange(call(blend_kernel, packed, own, near, far, tile))
    return call(
        unpack_kernel,
        jax.ShapeDtypeStruct((2, CHANNELS, ROWS, LON), BF16),
        returned,
        out_specs=pl.BlockSpec(memory_space=pl.ANY),
        scratch_shapes=[pltpu.VMEM((2, CHANNELS, ROWS, LON), BF16), pltpu.SemaphoreType.DMA((SLOTS // 2,))],
    )


def solution(mesh):
    in_specs = (
        P("member", None, "space", None),
        P(),
        P(),
        P(),
        P(),
        P("space", "member"),
        P("space", "member", None),
        P("space", "member", None),
        P("space", "member", None),
        P("space", "member", None),
    )
    out_specs = P("member", None, "space", None)
    return jax.shard_map(body, mesh=mesh, in_specs=in_specs, out_specs=out_specs, check_vma=False)
```

```python
import jax
import jax.numpy as jnp
from jax import lax
from jax.experimental import pallas as pl
from jax.experimental.pallas import tpu as pltpu
from jax.sharding import PartitionSpec as P

NS_STEPS = 6
NEAR_WEIGHT = 0.5
EPSILON = 1e-06
MEMBERS = 64
CHANNELS = 80
ROWS = 4
LON = 360
WIDE = 384
POINTS = 45
TILES = 32
BANDS = 8
PER_ROW = 8
SUB = 8
SLOTS = CHANNELS // SUB
PACK = 512
OBS = 256
HID = 320

F32 = jnp.float32
BF16 = jnp.bfloat16


def mm(left, right):
    return jnp.dot(left, right, preferred_element_type=F32)


def mm_t(left, right):
    return lax.dot_general(left, right, (((1,), (1,)), ((), ())), preferred_element_type=F32)


def halves(value):
    high = value.astype(BF16)
    return high, (value - high.astype(F32)).astype(BF16)


def mm_split(left, right, product=mm):
    left_high, left_low = halves(left)
    right_high, right_low = halves(right)
    return product(left_high, right_high) + (
        product(left_high, right_low) + product(left_low, right_high)
    )


def pieces(source, target, length):
    found = []
    done = 0
    while done < length:
        a, b = source + done, target + done
        step = min(length - done, 128 - a % 128, 128 - b % 128)
        found.append((a // 128, b // 128, (b - a) % 128, b % 128, b % 128 + step))
        done += step
    return found


def move(value, shift):
    return pltpu.roll(value, shift, 1) if shift else value


def shift_wrapped(west, here, east, lane):
    end = (LON - 1) % 128
    west_wrap = move(west[:, 256:], 128 - end)
    east_wrap = move(east[:, :128], end)
    west = pltpu.roll(west, 1, 1)
    east = pltpu.roll(east, WIDE - 1, 1)
    west = jnp.concatenate([jnp.where(lane == 0, west_wrap, west[:, :128]), west[:, 128:]], axis=1)
    east = jnp.concatenate([east[:, :256], jnp.where(lane == end, east_wrap, east[:, 256:])], axis=1)
    return here + west + east


def convolve(windows, conv):
    lane = lax.broadcasted_iota(jnp.int32, (CHANNELS, 128), 1)
    near, far = windows
    stacked = jnp.concatenate([jnp.concatenate([near[a], far[a]], axis=1) for a in range(3)], axis=0)
    taps = mm(conv, stacked)
    parts = []
    for d, window in enumerate(windows):
        west, here, east = [
            taps[CHANNELS * b : CHANNELS * (b + 1), WIDE * d : WIDE * (d + 1)] for b in range(3)
        ]
        parts.append(window[1].astype(F32) + shift_wrapped(west, here, east, lane))
    return jnp.concatenate(parts, axis=1)


def pointwise(updated, gain, first, second, held, m):
    power = jnp.sum(updated * updated, axis=0, keepdims=True) * (1.0 / CHANNELS)
    normed = (updated * lax.rsqrt(power + EPSILON) * gain).astype(BF16)
    hidden = mm(first, normed)
    hidden = (hidden * (0.5 + 0.5 * jnp.tanh(0.5 * hidden))).astype(BF16)
    result = updated + mm(second, hidden)
    held[0, m] = result[:, :WIDE]
    held[1, m] = result[:, WIDE:]


def pack_rows(held, starts, out_ref):
    spot = lax.broadcasted_iota(jnp.int32, (2 * SUB, 128), 1)
    for i, start in enumerate(starts):
        for j in range(PER_ROW):
            packed = [jnp.zeros((2 * SUB, 128), F32) for _ in range(PACK // 128)]
            for s in range(SLOTS):
                for a, b, shift, low, high in pieces(j * POINTS, s * POINTS, POINTS):
                    both = held[i, :, s * SUB : (s + 1) * SUB, a * 128 : (a + 1) * 128]
                    both = move(both.reshape(2 * SUB, 128), shift)
                    packed[b] = jnp.where((spot >= low) & (spot < high), both, packed[b])
            at = start + j * 2 * SUB
            out_ref[at : at + 2 * SUB, :] = jnp.concatenate(packed, axis=1).astype(BF16)


ROW_PACK = PER_ROW * 2 * SUB


def inner_kernel(
    x_ref,
    conv,
    first,
    second_ref,
    count,
    gain_hbm,
    point_hbm,
    channel_hbm,
    value_hbm,
    precision_hbm,
    out_ref,
    conv_ref,
    gain_ref,
    first_ref,
    obs_ref,
    bottom_ref,
    held,
    updated,
    gain,
    point,
    channel,
    value,
    precision,
    arrived,
):
    moves = [(gain_hbm, gain), (point_hbm, point), (channel_hbm, channel)]
    moves += [(value_hbm, value), (precision_hbm, precision)]
    copies = [pltpu.make_async_copy(source, target, arrived.at[i]) for i, (source, target) in enumerate(moves)]
    for copy in copies:
        copy.start()
    conv_ref[...] = jnp.concatenate(
        [conv[0, 3 * a : 3 * a + 3].reshape(3 * CHANNELS, CHANNELS) for a in range(3)], axis=1
    )
    first_ref[...] = first[...].astype(F32).T.astype(BF16)
    for m in range(2):
        updated[m] = convolve([[x_ref[m, r + d] for d in (-1, 0, 1)] for r in (1, 2)], conv_ref[...])
    copies[0].wait()
    row = lax.broadcasted_iota(jnp.int32, (CHANNELS, CHANNELS), 0)
    column = lax.broadcasted_iota(jnp.int32, (CHANNELS, CHANNELS), 1)
    tall = jnp.sum(jnp.where(row == column, gain[...], 0.0), axis=1, keepdims=True)
    gain_ref[...] = jnp.broadcast_to(tall, (CHANNELS, 128))
    for m in range(2):
        pointwise(updated[m], gain_ref[:, :1], first_ref[...], second_ref[...], held, m)
    pack_rows(held, (0, ROW_PACK), out_ref)
    bottom_ref[...] = x_ref[:, ROWS - 1]
    for copy in copies[1:]:
        copy.wait()
    slots = lax.broadcasted_iota(jnp.int32, (1, OBS), 1)
    obs_ref[0:1, :] = ((channel[...] // SUB) * POINTS + point[...]).astype(F32)
    obs_ref[1:2, :] = (channel[...] % SUB).astype(F32)
    obs_ref[2:3, :] = jnp.where(slots < count[...], precision[...], 0.0)
    obs_ref[3:4, :] = value[...]
    obs_ref[4:, :] = jnp.zeros((4, OBS), F32)


def outer_kernel(
    band_ref,
    x_ref,
    low_ref,
    high_ref,
    inner_ref,
    conv_ref,
    gain_ref,
    first_ref,
    second_ref,
    out_ref,
    held,
):
    band = band_ref[...]
    windows = []
    for m in range(2):
        low = jnp.where(band == 0, 0.0, low_ref[m].astype(F32)).astype(BF16)
        high = jnp.where(band == BANDS - 1, 0.0, high_ref[m].astype(F32)).astype(BF16)
        windows.append([[low, x_ref[m, 0], x_ref[m, 1]], [x_ref[m, 2], x_ref[m, 3], high]])
    for m in range(2):
        updated = convolve(windows[m], conv_ref[...])
        pointwise(updated, gain_ref[:, :1], first_ref[...], second_ref[...], held, m)
    pack_rows(held, (0, 3 * ROW_PACK), out_ref)
    out_ref[ROW_PACK : 3 * ROW_PACK, :] = inner_ref[...]


def observe_kernel(tile_ref, obs_ref, out_ref):
    place = lax.broadcasted_iota(jnp.int32, (PACK, OBS), 0)
    lane = obs_ref[0:1, :].astype(jnp.int32)
    sub = obs_ref[1:2, :].astype(jnp.int32)
    weight = obs_ref[2:3, :]
    found = mm(tile_ref[...], jnp.where(place == lane, 1.0, 0.0).astype(BF16))
    found = jnp.where(place % SUB == sub, found, 0.0)
    sampled = jnp.sum(found.reshape(MEMBERS, SUB, OBS), axis=1)
    average = jnp.sum(sampled, axis=0, keepdims=True) * (1.0 / MEMBERS)
    spread = sampled - average
    innovation = obs_ref[3:4, :] - average
    gram = mm_split(spread * weight, spread, mm_t)
    out_ref[: MEMBERS // 2, :MEMBERS] = gram[: MEMBERS // 2]
    out_ref[: MEMBERS // 2, MEMBERS:] = gram[MEMBERS // 2 :]
    pull = jnp.broadcast_to(weight * innovation, (8, OBS))
    out_ref[MEMBERS // 2 :, :MEMBERS] = mm_split(pull, spread, mm_t)
    out_ref[MEMBERS // 2 :, MEMBERS:] = jnp.zeros((8, MEMBERS), F32)


def blend_kernel(own_ref, near_ref, far_ref, tile_ref, out_ref):
    total = own_ref[...] + NEAR_WEIGHT * (near_ref[...] + far_ref[...])
    gram = jnp.concatenate([total[: MEMBERS // 2, :MEMBERS], total[: MEMBERS // 2, MEMBERS:]], axis=0)
    vector = total[MEMBERS // 2 : MEMBERS // 2 + 1, :MEMBERS]
    identity = jnp.where(
        lax.broadcasted_iota(jnp.int32, (MEMBERS, MEMBERS), 0)
        == lax.broadcasted_iota(jnp.int32, (MEMBERS, MEMBERS), 1),
        1.0,
        0.0,
    )
    system = (MEMBERS - 1.0) * identity + gram
    squares = jnp.sum(jnp.sum(system * system, axis=0, keepdims=True), axis=1, keepdims=True)
    scale = jnp.sqrt(squares)
    root = system / scale
    middle = 1.5 * identity - 0.5 * root
    root = mm_split(root, middle)
    inverse = middle
    for sweep in range(1, NS_STEPS):
        middle = 1.5 * identity - 0.5 * mm_split(inverse, root)
        if sweep < NS_STEPS - 1:
            root = mm_split(root, middle)
        inverse = mm_split(middle, inverse)
    once = jnp.sum(inverse * vector, axis=1, keepdims=True)
    mean_weight = jnp.sum(inverse * once, axis=0, keepdims=True) / scale
    full = jnp.sqrt((MEMBERS - 1.0) / scale) * inverse + mean_weight
    mixing = full + (1.0 - jnp.sum(full, axis=1, keepdims=True)) * (1.0 / MEMBERS)
    mixing = mixing.astype(BF16)
    spread_cols = jnp.where(
        lax.broadcasted_iota(jnp.int32, (MEMBERS, PACK), 1) // SUB
        == lax.broadcasted_iota(jnp.int32, (MEMBERS, PACK), 0),
        1.0,
        0.0,
    ).astype(BF16)
    wide = mm(mixing, spread_cols)
    square = jnp.broadcast_to(wide[:, None, :], (MEMBERS, SUB, PACK)).reshape(PACK, PACK)
    same = (
        lax.broadcasted_iota(jnp.int32, (PACK, PACK), 0) % SUB
        == lax.broadcasted_iota(jnp.int32, (PACK, PACK), 1) % SUB
    )
    square = jnp.where(same, square, 0.0).astype(BF16)
    out_ref[...] = mm(square, tile_ref[...]).astype(BF16)


def unpack_kernel(in_ref, out_hbm, laid, sent):
    spot = lax.broadcasted_iota(jnp.int32, (2 * SUB, 128), 1)
    copies = []
    for pair in range(SLOTS // 2):
        rows = []
        for r in range(ROWS):
            lines = []
            for s in (2 * pair, 2 * pair + 1):
                line = [jnp.zeros((2 * SUB, 128), F32) for _ in range(WIDE // 128)]
                for j in range(PER_ROW):
                    at = (r * PER_ROW + j) * 2 * SUB
                    for a, b, shift, low, high in pieces(s * POINTS, j * POINTS, POINTS):
                        both = in_ref[at : at + 2 * SUB, a * 128 : (a + 1) * 128].astype(F32)
                        line[b] = jnp.where((spot >= low) & (spot < high), move(both, shift), line[b])
                lines.append(jnp.concatenate(line, axis=1))
            rows.append(lines)
        block = slice(pair * 2 * SUB, (pair + 1) * 2 * SUB)
        for m in range(2):
            joined = [jnp.concatenate([line[m * SUB : (m + 1) * SUB] for line in lines], axis=0) for lines in rows]
            laid[m, block] = jnp.swapaxes(jnp.stack(joined), 0, 1)[:, :, :LON].astype(BF16)
        copies.append(pltpu.make_async_copy(laid.at[:, block], out_hbm.at[:, block], sent.at[pair]))
        copies[-1].start()
    for copy in copies:
        copy.wait()


def call(kernel, out_shape, *operands, **more):
    return pl.pallas_call(
        kernel,
        out_shape=out_shape,
        compiler_params=pltpu.CompilerParams(vmem_limit_bytes=40 * 1024 * 1024),
        **more,
    )(*operands)


def body(
    starting_fields,
    conv_weight,
    norm_gain,
    weight_in,
    weight_out,
    obs_count,
    obs_point,
    obs_channel,
    obs_value,
    obs_precision,
):
    fields = jnp.pad(starting_fields.transpose(0, 2, 1, 3), ((0, 0), (0, 0), (0, 0), (0, WIDE - LON)))
    fields = lax.optimization_barrier(fields)
    band = lax.axis_index("space")
    south = [((i + 1) % BANDS, i) for i in range(BANDS)]
    high = lax.ppermute(fields[:, 0], "space", south)
    held = [pltpu.VMEM((2, 2, CHANNELS, WIDE), F32)]
    second = weight_out[0]
    small = [
        (norm_gain, F32, (1, CHANNELS)),
        (obs_point[0], jnp.int32, (1, OBS)),
        (obs_channel[0], jnp.int32, (1, OBS)),
        (obs_value[0], F32, (1, OBS)),
        (obs_precision[0], F32, (1, OBS)),
    ]
    inner, conv, gain, first, observations, bottom = call(
        inner_kernel,
        (
            jax.ShapeDtypeStruct((2 * ROW_PACK, PACK), BF16),
            jax.ShapeDtypeStruct((3 * CHANNELS, 3 * CHANNELS), BF16),
            jax.ShapeDtypeStruct((CHANNELS, 128), F32),
            jax.ShapeDtypeStruct((HID, CHANNELS), BF16),
            jax.ShapeDtypeStruct((8, OBS), F32),
            jax.ShapeDtypeStruct((2, CHANNELS, WIDE), BF16),
        ),
        fields,
        conv_weight,
        weight_in[0].T,
        second,
        obs_count,
        *[pltpu.with_memory_space_constraint(array, pltpu.HBM) for array, _, _ in small],
        in_specs=[pl.BlockSpec(memory_space=pltpu.VMEM)] * 5 + [pl.BlockSpec(memory_space=pltpu.HBM)] * 5,
        scratch_shapes=held
        + [pltpu.VMEM((2, CHANNELS, 2 * WIDE), F32)]
        + [pltpu.VMEM(shape, kind) for _, kind, shape in small]
        + [pltpu.SemaphoreType.DMA((len(small),))],
        cost_estimate=pl.CostEstimate(flops=400_000_000, bytes_accessed=2_000_000, transcendentals=500_000),
    )
    weights = (conv, gain, first, second)
    low = lax.ppermute(bottom, "space", [(j, i) for i, j in south])
    packed = jax.ShapeDtypeStruct((PACK, PACK), BF16)
    sent = call(
        outer_kernel, packed, band.reshape(1, 1), fields, low, high, inner, *weights, scratch_shapes=held
    )

    def exchange(block):
        block = block.reshape(TILES, 2 * SUB, PACK)
        block = lax.all_to_all(block, "member", split_axis=0, concat_axis=0, tiled=True)
        return block.reshape(PACK, PACK)

    tile = exchange(sent)
    own = call(observe_kernel, jax.ShapeDtypeStruct((MEMBERS // 2 + 8, 128), F32), tile, observations)
    around = lax.axis_size("member")
    far = lax.ppermute(own, "member", [(i, (i + 1 if i % 2 else i - 1) % around) for i in range(around)])
    near = lax.ppermute(own, "member", [(i, i ^ 1) for i in range(around)])
    returned = exchange(call(blend_kernel, packed, own, near, far, tile))
    return call(
        unpack_kernel,
        jax.ShapeDtypeStruct((2, CHANNELS, ROWS, LON), BF16),
        returned,
        out_specs=pl.BlockSpec(memory_space=pl.ANY),
        scratch_shapes=[pltpu.VMEM((2, CHANNELS, ROWS, LON), BF16), pltpu.SemaphoreType.DMA((SLOTS // 2,))],
    )


def solution(mesh):
    in_specs = (
        P("member", None, "space", None),
        P(),
        P(),
        P(),
        P(),
        P("space", "member"),
        P("space", "member", None),
        P("space", "member", None),
        P("space", "member", None),
        P("space", "member", None),
    )
    out_specs = P("member", None, "space", None)
    return jax.shard_map(body, mesh=mesh, in_specs=in_specs, out_specs=out_specs, check_vma=False)
```

```python
import jax
import jax.numpy as jnp
from jax import lax
from jax.experimental import pallas as pl
from jax.experimental.pallas import tpu as pltpu
from jax.sharding import PartitionSpec as P

NS_STEPS = 6
NEAR_WEIGHT = 0.5
EPSILON = 1e-06
MEMBERS = 64
CHANNELS = 80
ROWS = 4
LON = 360
WIDE = 384
POINTS = 45
TILES = 32
BANDS = 8
PER_ROW = 8
SUB = 8
SLOTS = CHANNELS // SUB
PACK = 512
OBS = 256
HID = 320

F32 = jnp.float32
BF16 = jnp.bfloat16


def mm(left, right):
    return jnp.dot(left, right, preferred_element_type=F32)


def mm_t(left, right):
    return lax.dot_general(left, right, (((1,), (1,)), ((), ())), preferred_element_type=F32)


def halves(value):
    high = value.astype(BF16)
    return high, (value - high.astype(F32)).astype(BF16)


def mm_split(left, right, product=mm):
    left_high, left_low = halves(left)
    right_high, right_low = halves(right)
    return product(left_high, right_high) + (
        product(left_high, right_low) + product(left_low, right_high)
    )


def pieces(source, target, length):
    found = []
    done = 0
    while done < length:
        a, b = source + done, target + done
        step = min(length - done, 128 - a % 128, 128 - b % 128)
        found.append((a // 128, b // 128, (b - a) % 128, b % 128, b % 128 + step))
        done += step
    return found


def move(value, shift):
    return pltpu.roll(value, shift, 1) if shift else value


def shift_wrapped(west, here, east, lane):
    end = (LON - 1) % 128
    west_wrap = move(west[:, 256:], 128 - end)
    east_wrap = move(east[:, :128], end)
    west = pltpu.roll(west, 1, 1)
    east = pltpu.roll(east, WIDE - 1, 1)
    west = jnp.concatenate([jnp.where(lane == 0, west_wrap, west[:, :128]), west[:, 128:]], axis=1)
    east = jnp.concatenate([east[:, :256], jnp.where(lane == end, east_wrap, east[:, 256:])], axis=1)
    return here + west + east


def convolve(windows, conv):
    lane = lax.broadcasted_iota(jnp.int32, (CHANNELS, 128), 1)
    near, far = windows
    stacked = jnp.concatenate([jnp.concatenate([near[a], far[a]], axis=1) for a in range(3)], axis=0)
    taps = mm(conv, stacked)
    parts = []
    for d, window in enumerate(windows):
        west, here, east = [
            taps[CHANNELS * b : CHANNELS * (b + 1), WIDE * d : WIDE * (d + 1)] for b in range(3)
        ]
        parts.append(window[1].astype(F32) + shift_wrapped(west, here, east, lane))
    return jnp.concatenate(parts, axis=1)


def pointwise(updated, gain, first, second):
    power = jnp.sum(updated * updated, axis=0, keepdims=True) * (1.0 / CHANNELS)
    normed = (updated * lax.rsqrt(power + EPSILON) * gain).astype(BF16)
    hidden = mm(first, normed)
    hidden = (hidden * (0.5 + 0.5 * jnp.tanh(0.5 * hidden))).astype(BF16)
    return updated + mm(second, hidden)


def pack_rows(held, starts, out_ref):
    spot = lax.broadcasted_iota(jnp.int32, (2 * SUB, 128), 1)
    for i, start in enumerate(starts):
        for j in range(PER_ROW):
            packed = [jnp.zeros((2 * SUB, 128), F32) for _ in range(PACK // 128)]
            for s in range(SLOTS):
                for a, b, shift, low, high in pieces(j * POINTS, s * POINTS, POINTS):
                    both = held[i, :, s * SUB : (s + 1) * SUB, a * 128 : (a + 1) * 128]
                    both = move(both.reshape(2 * SUB, 128), shift)
                    packed[b] = jnp.where((spot >= low) & (spot < high), both, packed[b])
            at = start + j * 2 * SUB
            out_ref[at : at + 2 * SUB, :] = jnp.concatenate(packed, axis=1).astype(BF16)


ROW_PACK = PER_ROW * 2 * SUB


def inner_kernel(
    x_ref,
    conv,
    first,
    second_ref,
    count,
    gain_hbm,
    point_hbm,
    channel_hbm,
    value_hbm,
    precision_hbm,
    out_ref,
    conv_ref,
    gain_ref,
    first_ref,
    obs_ref,
    held,
    updated,
    gain,
    point,
    channel,
    value,
    precision,
    arrived,
):
    moves = [(gain_hbm, gain), (point_hbm, point), (channel_hbm, channel)]
    moves += [(value_hbm, value), (precision_hbm, precision)]
    copies = [pltpu.make_async_copy(source, target, arrived.at[i]) for i, (source, target) in enumerate(moves)]
    for copy in copies:
        copy.start()
    conv_ref[...] = jnp.concatenate(
        [conv[0, 3 * a : 3 * a + 3].reshape(3 * CHANNELS, CHANNELS) for a in range(3)], axis=1
    )
    first_ref[...] = first[...].astype(F32).T.astype(BF16)
    for m in range(2):
        updated[m] = convolve([[x_ref[m, r + d] for d in (-1, 0, 1)] for r in (1, 2)], conv_ref[...])
    copies[0].wait()
    row = lax.broadcasted_iota(jnp.int32, (CHANNELS, CHANNELS), 0)
    column = lax.broadcasted_iota(jnp.int32, (CHANNELS, CHANNELS), 1)
    tall = jnp.sum(jnp.where(row == column, gain[...], 0.0), axis=1, keepdims=True)
    gain_ref[...] = jnp.broadcast_to(tall, (CHANNELS, 128))
    for m in range(2):
        result = pointwise(updated[m], gain_ref[:, :1], first_ref[...], second_ref[...])
        held[0, m] = result[:, :WIDE]
        held[1, m] = result[:, WIDE:]
    pack_rows(held, (0, ROW_PACK), out_ref)
    for copy in copies[1:]:
        copy.wait()
    slots = lax.broadcasted_iota(jnp.int32, (1, OBS), 1)
    obs_ref[0:1, :] = ((channel[...] // SUB) * POINTS + point[...]).astype(F32)
    obs_ref[1:2, :] = (channel[...] % SUB).astype(F32)
    obs_ref[2:3, :] = jnp.where(slots < count[...], precision[...], 0.0)
    obs_ref[3:4, :] = value[...]
    obs_ref[4:, :] = jnp.zeros((4, OBS), F32)


def edge_rows(windows, conv_ref, gain_ref, first_ref, second_ref, held, out_ref, start):
    updated = convolve(windows, conv_ref[...])
    gain = gain_ref[:, :1]
    result = pointwise(updated, gain, first_ref[...], second_ref[...])
    for m in range(2):
        held[0, m] = result[:, m * WIDE : (m + 1) * WIDE]
    pack_rows(held, (start,), out_ref)


def either(choice, left, right):
    return jnp.where(choice, left.astype(F32), right.astype(F32)).astype(BF16)


def chip_kernel(band_ref, x_ref, chip_ref, conv_ref, gain_ref, first_ref, second_ref, out_ref, held):
    odd = band_ref[...] % 2 == 1
    windows = []
    for m in range(2):
        above = either(odd, chip_ref[m], x_ref[m, ROWS - 2])
        here = either(odd, x_ref[m, 0], x_ref[m, ROWS - 1])
        below = either(odd, x_ref[m, 1], chip_ref[m])
        windows.append([above, here, below])
    edge_rows(windows, conv_ref, gain_ref, first_ref, second_ref, held, out_ref, 0)


def next_kernel(
    band_ref, x_ref, next_ref, inner_ref, chip_ref, conv_ref, gain_ref, first_ref, second_ref, out_ref, held, edge
):
    band = band_ref[...]
    odd = band % 2 == 1
    outside = (band == 0) | (band == BANDS - 1)
    windows = []
    for m in range(2):
        beyond = jnp.where(outside, 0.0, next_ref[m].astype(F32)).astype(BF16)
        above = either(odd, x_ref[m, ROWS - 2], beyond)
        here = either(odd, x_ref[m, ROWS - 1], x_ref[m, 0])
        below = either(odd, beyond, x_ref[m, 1])
        windows.append([above, here, below])
    edge_rows(windows, conv_ref, gain_ref, first_ref, second_ref, held, edge, 0)
    out_ref[:ROW_PACK, :] = either(odd, chip_ref[...], edge[...])
    out_ref[ROW_PACK : 3 * ROW_PACK, :] = inner_ref[...]
    out_ref[3 * ROW_PACK :, :] = either(odd, edge[...], chip_ref[...])


def observe_kernel(tile_ref, obs_ref, out_ref):
    place = lax.broadcasted_iota(jnp.int32, (PACK, OBS), 0)
    lane = obs_ref[0:1, :].astype(jnp.int32)
    sub = obs_ref[1:2, :].astype(jnp.int32)
    weight = obs_ref[2:3, :]
    found = mm(tile_ref[...], jnp.where(place == lane, 1.0, 0.0).astype(BF16))
    found = jnp.where(place % SUB == sub, found, 0.0)
    sampled = jnp.sum(found.reshape(MEMBERS, SUB, OBS), axis=1)
    average = jnp.sum(sampled, axis=0, keepdims=True) * (1.0 / MEMBERS)
    spread = sampled - average
    innovation = obs_ref[3:4, :] - average
    gram = mm_split(spread * weight, spread, mm_t)
    out_ref[: MEMBERS // 2, :MEMBERS] = gram[: MEMBERS // 2]
    out_ref[: MEMBERS // 2, MEMBERS:] = gram[MEMBERS // 2 :]
    pull = jnp.broadcast_to(weight * innovation, (8, OBS))
    out_ref[MEMBERS // 2 :, :MEMBERS] = mm_split(pull, spread, mm_t)
    out_ref[MEMBERS // 2 :, MEMBERS:] = jnp.zeros((8, MEMBERS), F32)


def blend_kernel(own_ref, near_ref, far_ref, tile_ref, out_ref):
    total = own_ref[...] + NEAR_WEIGHT * (near_ref[...] + far_ref[...])
    gram = jnp.concatenate([total[: MEMBERS // 2, :MEMBERS], total[: MEMBERS // 2, MEMBERS:]], axis=0)
    vector = total[MEMBERS // 2 : MEMBERS // 2 + 1, :MEMBERS]
    identity = jnp.where(
        lax.broadcasted_iota(jnp.int32, (MEMBERS, MEMBERS), 0)
        == lax.broadcasted_iota(jnp.int32, (MEMBERS, MEMBERS), 1),
        1.0,
        0.0,
    )
    system = (MEMBERS - 1.0) * identity + gram
    squares = jnp.sum(jnp.sum(system * system, axis=0, keepdims=True), axis=1, keepdims=True)
    scale = jnp.sqrt(squares)
    root = system / scale
    middle = 1.5 * identity - 0.5 * root
    root = mm_split(root, middle)
    inverse = middle
    for sweep in range(1, NS_STEPS):
        middle = 1.5 * identity - 0.5 * mm_split(inverse, root)
        if sweep < NS_STEPS - 1:
            root = mm_split(root, middle)
        inverse = mm_split(middle, inverse)
    once = jnp.sum(inverse * vector, axis=1, keepdims=True)
    mean_weight = jnp.sum(inverse * once, axis=0, keepdims=True) / scale
    full = jnp.sqrt((MEMBERS - 1.0) / scale) * inverse + mean_weight
    mixing = full + (1.0 - jnp.sum(full, axis=1, keepdims=True)) * (1.0 / MEMBERS)
    mixing = mixing.astype(BF16)
    spread_cols = jnp.where(
        lax.broadcasted_iota(jnp.int32, (MEMBERS, PACK), 1) // SUB
        == lax.broadcasted_iota(jnp.int32, (MEMBERS, PACK), 0),
        1.0,
        0.0,
    ).astype(BF16)
    wide = mm(mixing, spread_cols)
    square = jnp.broadcast_to(wide[:, None, :], (MEMBERS, SUB, PACK)).reshape(PACK, PACK)
    same = (
        lax.broadcasted_iota(jnp.int32, (PACK, PACK), 0) % SUB
        == lax.broadcasted_iota(jnp.int32, (PACK, PACK), 1) % SUB
    )
    square = jnp.where(same, square, 0.0).astype(BF16)
    out_ref[...] = mm(square, tile_ref[...]).astype(BF16)


def unpack_kernel(in_ref, out_hbm, laid, sent):
    spot = lax.broadcasted_iota(jnp.int32, (2 * SUB, 128), 1)
    copies = []
    for pair in range(SLOTS // 2):
        rows = []
        for r in range(ROWS):
            lines = []
            for s in (2 * pair, 2 * pair + 1):
                line = [jnp.zeros((2 * SUB, 128), F32) for _ in range(WIDE // 128)]
                for j in range(PER_ROW):
                    at = (r * PER_ROW + j) * 2 * SUB
                    for a, b, shift, low, high in pieces(s * POINTS, j * POINTS, POINTS):
                        both = in_ref[at : at + 2 * SUB, a * 128 : (a + 1) * 128].astype(F32)
                        line[b] = jnp.where((spot >= low) & (spot < high), move(both, shift), line[b])
                lines.append(jnp.concatenate(line, axis=1))
            rows.append(lines)
        block = slice(pair * 2 * SUB, (pair + 1) * 2 * SUB)
        for m in range(2):
            joined = [jnp.concatenate([line[m * SUB : (m + 1) * SUB] for line in lines], axis=0) for lines in rows]
            laid[m, block] = jnp.swapaxes(jnp.stack(joined), 0, 1)[:, :, :LON].astype(BF16)
        copies.append(pltpu.make_async_copy(laid.at[:, block], out_hbm.at[:, block], sent.at[pair]))
        copies[-1].start()
    for copy in copies:
        copy.wait()


def call(kernel, out_shape, *operands, **more):
    return pl.pallas_call(
        kernel,
        out_shape=out_shape,
        compiler_params=pltpu.CompilerParams(vmem_limit_bytes=40 * 1024 * 1024),
        **more,
    )(*operands)


def body(
    starting_fields,
    conv_weight,
    norm_gain,
    weight_in,
    weight_out,
    obs_count,
    obs_point,
    obs_channel,
    obs_value,
    obs_precision,
):
    fields = jnp.pad(starting_fields.transpose(0, 2, 1, 3), ((0, 0), (0, 0), (0, 0), (0, WIDE - LON)))
    fields = lax.optimization_barrier(fields)
    band = lax.axis_index("space")
    odd = band % 2
    top, bottom = fields[:, 0], fields[:, ROWS - 1]
    across = [(i, (i + 1 if i % 2 else i - 1) % BANDS) for i in range(BANDS)]
    next_row = lax.ppermute(jnp.where(odd == 1, bottom, top), "space", across)
    within = [(i, i ^ 1) for i in range(BANDS)]
    chip_row = lax.ppermute(jnp.where(odd == 1, top, bottom), "space", within)
    held = [pltpu.VMEM((2, 2, CHANNELS, WIDE), F32)]
    second = weight_out[0]
    small = [
        (norm_gain, F32, (1, CHANNELS)),
        (obs_point[0], jnp.int32, (1, OBS)),
        (obs_channel[0], jnp.int32, (1, OBS)),
        (obs_value[0], F32, (1, OBS)),
        (obs_precision[0], F32, (1, OBS)),
    ]
    inner, conv, gain, first, observations = call(
        inner_kernel,
        (
            jax.ShapeDtypeStruct((2 * ROW_PACK, PACK), BF16),
            jax.ShapeDtypeStruct((3 * CHANNELS, 3 * CHANNELS), BF16),
            jax.ShapeDtypeStruct((CHANNELS, 128), F32),
            jax.ShapeDtypeStruct((HID, CHANNELS), BF16),
            jax.ShapeDtypeStruct((8, OBS), F32),
        ),
        fields,
        conv_weight,
        weight_in[0].T,
        second,
        obs_count,
        *[pltpu.with_memory_space_constraint(array, pltpu.HBM) for array, _, _ in small],
        in_specs=[pl.BlockSpec(memory_space=pltpu.VMEM)] * 5 + [pl.BlockSpec(memory_space=pltpu.HBM)] * 5,
        scratch_shapes=held
        + [pltpu.VMEM((2, CHANNELS, 2 * WIDE), F32)]
        + [pltpu.VMEM(shape, kind) for _, kind, shape in small]
        + [pltpu.SemaphoreType.DMA((len(small),))],
        cost_estimate=pl.CostEstimate(flops=400_000_000, bytes_accessed=2_000_000, transcendentals=500_000),
    )
    weights = (conv, gain, first, second)
    packed = jax.ShapeDtypeStruct((PACK, PACK), BF16)
    band = band.reshape(1, 1)
    beside = call(
        chip_kernel,
        jax.ShapeDtypeStruct((ROW_PACK, PACK), BF16),
        band,
        fields,
        chip_row,
        *weights,
        scratch_shapes=held,
        cost_estimate=pl.CostEstimate(flops=200_000_000, bytes_accessed=1_000_000, transcendentals=250_000),
    )
    sent = call(
        next_kernel,
        packed,
        band,
        fields,
        next_row,
        inner,
        beside,
        *weights,
        scratch_shapes=held + [pltpu.VMEM((ROW_PACK, PACK), BF16)],
    )

    def exchange(block):
        block = block.reshape(TILES, 2 * SUB, PACK)
        block = lax.all_to_all(block, "member", split_axis=0, concat_axis=0, tiled=True)
        return block.reshape(PACK, PACK)

    tile = exchange(sent)
    own = call(observe_kernel, jax.ShapeDtypeStruct((MEMBERS // 2 + 8, 128), F32), tile, observations)
    around = lax.axis_size("member")
    far = lax.ppermute(own, "member", [(i, (i + 1 if i % 2 else i - 1) % around) for i in range(around)])
    near = lax.ppermute(own, "member", [(i, i ^ 1) for i in range(around)])
    returned = exchange(call(blend_kernel, packed, own, near, far, tile))
    return call(
        unpack_kernel,
        jax.ShapeDtypeStruct((2, CHANNELS, ROWS, LON), BF16),
        returned,
        out_specs=pl.BlockSpec(memory_space=pl.ANY),
        scratch_shapes=[pltpu.VMEM((2, CHANNELS, ROWS, LON), BF16), pltpu.SemaphoreType.DMA((SLOTS // 2,))],
    )


def solution(mesh):
    in_specs = (
        P("member", None, "space", None),
        P(),
        P(),
        P(),
        P(),
        P("space", "member"),
        P("space", "member", None),
        P("space", "member", None),
        P("space", "member", None),
        P("space", "member", None),
    )
    out_specs = P("member", None, "space", None)
    return jax.shard_map(body, mesh=mesh, in_specs=in_specs, out_specs=out_specs, check_vma=False)
```
